32 devices in a mesh: member: 8 (over y, x, core), tile: 4 (over z).
Axes of the slice: x: 2, y: 2, z: 4, core: 2. Of those that a mesh axis runs over, the one named last changes fastest.
Arguments:
- prior_state: float32 [16, 10, 64, 1024], P('member', None, 'tile'), may hold values from -8 to 8
- velocity: float32 [16, 4, 64, 1024], P('member', None, 'tile'), may hold values from -0.3 to 0.3
- band_bins: int32 [64, 1024], P('tile'), may hold values from 0 to 3
- settle_table: float32 [4, 4], replicated, may hold values from 0.05 to 0.5
- measure_latitude: int32 [16], replicated, may hold values from 2 to 62
- measure_longitude: int32 [16], replicated, may hold values from 64 to 960
- obs_layer: int32 [16], replicated, may hold values from 0 to 1
- obs_kind: int32 [16], replicated, may hold values from 0 to 4
- obs_value: float32 [16], replicated, may hold values from 0 to 2
- obs_error: float32 [16], replicated, may hold values from 0.2 to 1
- obs_perturb: float32 [16, 16], P('member'), may hold values from -5 to 5
Outputs:
- analysis: float32 [16, 10, 64, 1024], P('member', None, 'tile')
The draws below stay inside these ranges and needn't reach their ends.
All inputs are finite; a program needn't handle non-finite values.
Results may differ from the reference program's by a relative error of at most 0.000061.
Values sent between devices are 32-bit elements; how exact they have to be, the bound alone decides.
No kernel may reach another device: no remote copies, remote signals or barrier semaphores. Data moves between devices by JAX's collectives and lax.ppermute only.
A program may use at most 192 MiB of HBM per device.

```python
import math
import jax
import jax.numpy as jnp
from jax import lax

MESH_WIDTH = 1024
NLAYER = 2
NCLASS = 4
NBAND = 4
MEASURE_COUNT = 16
WINDOW_HEIGHT = 4
WINDOW_WIDTH = 128
SUBSTEPS = 2
EVOLVED_SLOTS = 10
REPLICA_COUNT = 16
MESH_HEIGHT = 64


row_factors = (4.0, 5.0, 6.0, 8.0)


col_factors = (4.0, 6.0, 5.0, 8.0)


def smooth_modes(key, amplitude, rough_lo, rough_hi):
    phase_key, shift_key, rough_key = jax.random.split(key, 3)
    phase_rows = jax.random.uniform(phase_key, (REPLICA_COUNT, 1, 4), jnp.float32, 0.0, 2.0 * math.pi)
    phase_cols = jax.random.uniform(shift_key, (REPLICA_COUNT, 1, 4), jnp.float32, 0.0, 2.0 * math.pi)
    row_axis = jnp.arange(MESH_HEIGHT, dtype=jnp.float32)
    col_axis = jnp.arange(MESH_WIDTH, dtype=jnp.float32)
    total = jnp.zeros((REPLICA_COUNT, EVOLVED_SLOTS, MESH_HEIGHT, MESH_WIDTH), jnp.float32)
    for index in range(4):
        row_wave = jnp.cos(2.0 * math.pi * row_axis[None, None, :] / (row_factors[index] * WINDOW_HEIGHT) + phase_rows[:, :, index:index + 1])
        col_wave = jnp.cos(2.0 * math.pi * col_axis[None, None, :] / (col_factors[index] * WINDOW_WIDTH) + phase_cols[:, :, index:index + 1])
        total = total + amplitude[:, :, index, None, None] * row_wave[:, :, :, None] * col_wave[:, :, None, :]
    rough = jax.random.uniform(rough_key, (REPLICA_COUNT, EVOLVED_SLOTS, MESH_HEIGHT, MESH_WIDTH), jnp.float32, rough_lo, rough_hi)
    return rough * total


def draw_prior_state(key, part):
    key = jax.random.fold_in(key, 11)
    base_key, common_key, own_key, mode_key = jax.random.split(key, 4)
    common = jax.random.normal(common_key, (REPLICA_COUNT, 1, 4), jnp.float32)
    own = jax.random.normal(own_key, (REPLICA_COUNT, EVOLVED_SLOTS, 4), jnp.float32)
    amplitude = 0.8 * common + 0.6 * own
    base = jax.random.uniform(base_key, (1, EVOLVED_SLOTS, MESH_HEIGHT, MESH_WIDTH), jnp.float32, 0.25, 0.75)
    spread = smooth_modes(mode_key, amplitude, 0.5, 1.5)
    return jnp.clip(base + 1.2 * spread, -8.0, 8.0)


def set_ends(result, stream_key, smallest, high):
    place = [jax.random.randint(jax.random.fold_in(stream_key, axis), (), 0, length) for axis, length in enumerate(result.shape)]
    widest = result.shape.index(max(result.shape))
    next_to = place[:widest] + [(place[widest] + 1) % result.shape[widest]] + place[widest + 1:]
    return result.at[tuple(place)].set(smallest).at[tuple(next_to)].set(high)


def block_levels(key, dims, shards, least, largest):
    def one(position, shards_of):
        draws = jax.random.uniform(jax.random.fold_in(jax.random.fold_in(key, 6), position), (shards_of,), jnp.float32, least / len(shards), largest / len(shards))
        return jnp.repeat(jnp.exp(draws), dims[position] // shards_of).reshape((-1,) + (1,) * (len(dims) - position - 1))

    level = one(*shards[0])
    for cut in shards[1:]:
        level = level * one(*cut)
    return level


def bell_draw(stream_key, extent, deviation, bound, pieces=(), kind=jnp.bfloat16):
    array = jax.random.normal(stream_key, extent, jnp.float32) * deviation
    if len(pieces) > 0:
        array = block_levels(stream_key, extent, pieces, -0.22, 0.18) * array
    return jnp.clip(array, min=-bound, max=bound).astype(kind)


def setup_inputs(seed: int = 0) -> dict:
    key_of = jax.random.split(jax.random.key(seed), 12)
    return {
        "prior_state": draw_prior_state(jax.random.fold_in(key_of[11], 71), 0),
        "velocity": jnp.clip(jax.random.uniform(key_of[1], (REPLICA_COUNT, 2 * NLAYER, MESH_HEIGHT, MESH_WIDTH), jnp.float32, -0.3, 0.3) * block_levels(key_of[1], (REPLICA_COUNT, 2 * NLAYER, MESH_HEIGHT, MESH_WIDTH), ((0, 8), (2, 4)), -0.4, 0.0), -0.3, 0.3),
        "band_bins": set_ends(jax.random.randint(key_of[2], (MESH_HEIGHT, MESH_WIDTH), 0, NBAND), jax.random.fold_in(key_of[2], 1), 0, NBAND - 1).astype(jnp.int32),
        "settle_table": jnp.clip(jnp.exp(jax.random.uniform(key_of[3], (NBAND, NCLASS), jnp.float32, math.log(0.05), math.log(0.5))), 0.05, 0.5),
        "measure_latitude": set_ends(jax.random.randint(key_of[4], (MEASURE_COUNT,), WINDOW_HEIGHT // 2, MESH_HEIGHT - WINDOW_HEIGHT // 2 + 1), jax.random.fold_in(key_of[4], 1), WINDOW_HEIGHT // 2, (MESH_HEIGHT - WINDOW_HEIGHT // 2 + 1) - 1).astype(jnp.int32),
        "measure_longitude": set_ends(jax.random.randint(key_of[5], (MEASURE_COUNT,), WINDOW_WIDTH // 2, MESH_WIDTH - WINDOW_WIDTH // 2 + 1), jax.random.fold_in(key_of[5], 1), WINDOW_WIDTH // 2, (MESH_WIDTH - WINDOW_WIDTH // 2 + 1) - 1).astype(jnp.int32),
        "obs_layer": set_ends(jax.random.randint(key_of[6], (MEASURE_COUNT,), 0, NLAYER), jax.random.fold_in(key_of[6], 1), 0, NLAYER - 1).astype(jnp.int32),
        "obs_kind": set_ends(jax.random.randint(key_of[7], (MEASURE_COUNT,), 0, NCLASS + 1), jax.random.fold_in(key_of[7], 1), 0, NCLASS).astype(jnp.int32),
        "obs_value": jnp.clip(jax.random.uniform(key_of[8], (MEASURE_COUNT,), jnp.float32, 0.0, 2.0), 0.0, 2.0),
        "obs_error": jnp.clip(jnp.exp(jax.random.uniform(key_of[9], (MEASURE_COUNT,), jnp.float32, math.log(0.2), math.log(1.0))), 0.2, 1.0),
        "obs_perturb": bell_draw(key_of[10], (REPLICA_COUNT, MEASURE_COUNT), 1.0, 5.0, ((0, 8),), jnp.float32),
    }


DIFFUSION = 0.08
DEPOSIT = 0.5

def transport(suspended_concentration, zonal_cfl_ratio, meridional_cfl_ratio):
    centre = suspended_concentration[..., 1:-1, :]
    upper_row = suspended_concentration[..., :-2, :]
    lower_row = suspended_concentration[..., 2:, :]
    widths = [(0, 0)] * (centre.ndim - 1) + [(1, 1)]
    widened = jnp.pad(centre, widths)
    left_cells = widened[..., :-2]
    right_cells = widened[..., 2:]
    advected = jnp.maximum(zonal_cfl_ratio, 0.0) * (centre - upper_row) + jnp.minimum(zonal_cfl_ratio, 0.0) * (lower_row - centre) + jnp.maximum(meridional_cfl_ratio, 0.0) * (centre - left_cells) + jnp.minimum(meridional_cfl_ratio, 0.0) * (right_cells - centre)
    laplace = upper_row + lower_row + left_cells + right_cells - 4.0 * centre
    return centre - advected + DIFFUSION * laplace

def deposition_advance(suspended_concentration, fall_speed):
    top_layer = suspended_concentration[..., 0, 1:, :, :]
    bottom = suspended_concentration[..., 1, 1:, :, :]
    settled = fall_speed * top_layer
    new_top = jnp.concatenate([suspended_concentration[..., 0, :1, :, :], top_layer - settled], axis=-3)
    new_bottom = jnp.concatenate([suspended_concentration[..., 1, :1, :, :], bottom + settled - DEPOSIT * fall_speed * bottom], axis=-3)
    return jnp.stack([new_top, new_bottom], axis=-4)

def class_rates(band_bins, settle_table):
    levels = jnp.arange(settle_table.shape[0], dtype=jnp.int32)
    onehot = (band_bins[None] == levels[:, None, None]).astype(jnp.float32)
    return lax.optimization_barrier(jnp.sum(settle_table[:, :, None, None] * onehot[:, None], axis=0))

def taper_table(patch_rows, patch_cols):
    row_pos = (jnp.arange(patch_rows, dtype=jnp.float32) + 0.5 - patch_rows / 2) / (patch_rows / 2)
    col_pos = (jnp.arange(patch_cols, dtype=jnp.float32) + 0.5 - patch_cols / 2) / (patch_cols / 2)
    return (1.0 - row_pos * row_pos)[:, None] * (1.0 - col_pos * col_pos)[None, :]

def reference(prior_state, velocity, band_bins, settle_table, measure_latitude, measure_longitude, obs_layer, obs_kind, obs_value, obs_error, obs_perturb):
    fall_speed = class_rates(band_bins, settle_table)
    zonal_cfl_ratio = velocity[:, 0::2, None]
    meridional_cfl_ratio = velocity[:, 1::2, None]
    arranged_vector = prior_state.reshape(REPLICA_COUNT, NLAYER, NCLASS + 1, MESH_HEIGHT, MESH_WIDTH)

    def prior_replica(replica_vectors):
        suspended_concentration, u_one, v_one = replica_vectors
        for substep in range(SUBSTEPS):
            haloed_vector = jnp.pad(suspended_concentration, ((0, 0), (0, 0), (1, 1), (0, 0)))
            suspended_concentration = transport(haloed_vector, u_one, v_one)
        return deposition_advance(suspended_concentration, fall_speed)
    prior_replicas = lax.map(prior_replica, (arranged_vector, zonal_cfl_ratio, meridional_cfl_ratio)).reshape(REPLICA_COUNT, EVOLVED_SLOTS, MESH_HEIGHT, MESH_WIDTH)
    quantity_ordinal = obs_layer * (NCLASS + 1) + obs_kind
    measured_data = prior_replicas[:, quantity_ordinal, measure_latitude, measure_longitude]
    starts_r = (measure_latitude - WINDOW_HEIGHT // 2).astype(jnp.int32)
    starts_c = (measure_longitude - WINDOW_WIDTH // 2).astype(jnp.int32)
    window_offset = jnp.zeros((), jnp.int32)

    def cut_patch(window_first_latitude, window_first_longitude):
        return lax.dynamic_slice(prior_replicas, (window_offset, window_offset, window_first_latitude, window_first_longitude), (REPLICA_COUNT, EVOLVED_SLOTS, WINDOW_HEIGHT, WINDOW_WIDTH))
    patches = jax.vmap(cut_patch)(starts_r, starts_c)
    mean_obs = lax.optimization_barrier(jnp.mean(measured_data, axis=0))
    anomaly = measured_data - mean_obs
    cov_obs = jnp.dot(anomaly.T, anomaly, precision=lax.Precision.HIGHEST)
    cov_cross = lax.optimization_barrier(jnp.sum(patches * anomaly.T[:, :, None, None, None], axis=1))
    system = cov_obs / (REPLICA_COUNT - 1) + jnp.diag(obs_error)
    factor = jnp.linalg.cholesky(system)
    innovation = obs_value[None] + jnp.sqrt(obs_error)[None] * obs_perturb - measured_data
    weights_obs = jax.scipy.linalg.cho_solve((factor, True), innovation.T)
    gain = taper_table(WINDOW_HEIGHT, WINDOW_WIDTH) * cov_cross / (REPLICA_COUNT - 1)

    def write_window_increment(obs_index, analysed):
        increment = gain[obs_index][None] * weights_obs[obs_index][:, None, None, None]
        corner = (window_offset, window_offset, starts_r[obs_index], starts_c[obs_index])
        current = lax.dynamic_slice(analysed, corner, increment.shape)
        return lax.dynamic_update_slice(analysed, current + increment, corner)
    return lax.fori_loop(0, MEASURE_COUNT, write_window_increment, prior_replicas)
```

```python
import functools

import jax
import jax.numpy as jnp
from jax import lax
from jax.experimental import pallas as pl
from jax.experimental.pallas import tpu as pltpu
from jax.sharding import PartitionSpec as P

NLAYER = 2
NCLASS = 4
KINDS = NCLASS + 1
FIELDS = NLAYER * KINDS
WINDOW_HEIGHT = 4
WINDOW_WIDTH = 128
DIFFUSION = 0.08
DEPOSIT = 0.5

LANES = 128
PAD = 8
GROUP = 8
NEAR_BLOCKS = 12
EXACT = lax.Precision.HIGHEST
MIB = 1024 * 1024

SMEM = pl.BlockSpec(memory_space=pltpu.SMEM)
VMEM = pl.BlockSpec(memory_space=pltpu.VMEM)


def call(kernel, name, in_specs, outs, scratch=(), flops=1000000):
    return pl.pallas_call(
        kernel,
        name=name,
        in_specs=in_specs,
        out_specs=[VMEM] * len(outs),
        out_shape=[jax.ShapeDtypeStruct(shape, jnp.float32) for shape in outs],
        scratch_shapes=list(scratch),
        compiler_params=pltpu.CompilerParams(vmem_limit_bytes=40 * MIB),
        cost_estimate=pl.CostEstimate(flops=flops, bytes_accessed=1000000, transcendentals=0),
    )


def lane_index(rows=8):
    return lax.broadcasted_iota(jnp.int32, (rows, LANES), 1)


def row_index(rows=8):
    return lax.broadcasted_iota(jnp.int32, (rows, LANES), 0)


def spread(ref, group, rows=8):
    index = lane_index(rows) // group
    total = jnp.zeros((rows, LANES), ref.dtype)
    for j in range(ref.shape[0]):
        total = jnp.where(index == j, ref[j], total)
    return total


def find_slots(lat, slots, first, rows, cap):
    for s in range(cap + 1):
        slots[s] = 0
    count = jnp.int32(0)
    for j in range(lat.shape[0]):
        start = lat[j] - WINDOW_HEIGHT // 2 - first
        slots[jnp.minimum(count, cap)] = j
        count = count + ((start < rows) & (start + WINDOW_HEIGHT > 0)).astype(jnp.int32)
    return jnp.minimum(count, cap)


def window(lat, lon, j, first, rows, tiles):
    row = jnp.clip(lat[j] - WINDOW_HEIGHT // 2 - first, -WINDOW_HEIGHT, rows) + PAD
    left = lon[j] - WINDOW_WIDTH // 2
    block = left // LANES
    return row, block, jnp.minimum(block + 1, tiles - 1), left % LANES


def coefficients(u, w):
    return (
        (1.0 - 4.0 * DIFFUSION) - (jnp.abs(u) + jnp.abs(w)),
        jnp.maximum(u, 0.0) + DIFFUSION,
        DIFFUSION - jnp.minimum(u, 0.0),
        jnp.maximum(w, 0.0) + DIFFUSION,
        DIFFUSION - jnp.minimum(w, 0.0),
    )


def stencil(coef, centre, up, down, left, right):
    return (coef[0] * centre + coef[1] * up) + (coef[2] * down + coef[3] * left) + coef[4] * right


def pack_kernel(lat, lon, kind, state, vel, band, out_a, out_b, near):
    members, _, rows, width = state.shape
    tiles = width // LANES
    tile = lax.axis_index("tile")
    even = tile % 2 == 0
    per = members * (2 * FIELDS + 2 * NLAYER)

    def edge(out, row, vrow):
        for i in range(tiles):
            lanes = slice(i * LANES, (i + 1) * LANES)
            for m in range(members):
                for f in range(FIELDS):
                    to = i * per + (m * FIELDS + f) * 2
                    out[to : to + 2, :] = state[m, f, row : row + 2, lanes]
                for c in range(2 * NLAYER):
                    to = i * per + members * FIELDS * 2 + m * 2 * NLAYER + c
                    out[to : to + 1, :] = vel[m, c, vrow : vrow + 1, lanes]

    @pl.when(even)
    def _():
        edge(out_a, rows - 2, rows - 1)
        edge(out_b, 0, 0)

    @pl.when(jnp.logical_not(even))
    def _():
        edge(out_a, 0, 0)
        edge(out_b, rows - 2, rows - 1)

    first = tile * rows
    latv = spread(lat, GROUP, rows)
    kindv = spread(kind, GROUP, rows)
    lonv = spread(lon, GROUP, 8)[:1]
    column = lonv - 2 + (lane_index(8)[:1] % GROUP)
    pick = (lax.broadcasted_iota(jnp.int32, (width, LANES), 0) == column).astype(jnp.float32)

    def chosen(array, lead):
        flat = array.reshape(lead * rows, width)
        out = jnp.dot(flat, pick, precision=EXACT, preferred_element_type=jnp.float32)
        return [out[n * rows : (n + 1) * rows] for n in range(lead)]

    qs = chosen(state[...], members * FIELDS)
    vs = chosen(vel[...], members * 2 * NLAYER)
    bs = chosen(band[...].astype(jnp.float32), 1)
    near[...] = jnp.zeros(near.shape, jnp.float32)
    at = row_index(rows) + first - latv

    def put(block, s, offset, values):
        row = jnp.sum(jnp.where(at == offset, values, 0.0), axis=0, keepdims=True)
        near[block * 8 + s : block * 8 + s + 1, :] = row

    for m in range(members):
        for l in range(NLAYER):
            s = m * NLAYER + l
            q = jnp.zeros((rows, LANES), jnp.float32)
            for k in range(KINDS):
                q = jnp.where(kindv == k, qs[m * FIELDS + l * KINDS + k], q)
            for i in range(5):
                put(i, s, i - 2, q)
            for c in range(2):
                for i in range(3):
                    put(5 + 3 * c + i, s, i - 1, vs[m * 2 * NLAYER + 2 * l + c])
    put(11, 0, 0, bs[0])
    base = tiles * per
    out_a[base : base + NEAR_BLOCKS * 8, :] = near[...]


def forecast_kernel(cap, others, lat, lon, layer, kind, table, state, vel, band, from_a, from_b, *rest):
    nears, rest = rest[: 1 + others], rest[1 + others :]
    out, own, send, obs_out, sel, s0, s1, vs, padded, slots = rest
    members, _, rows, width = state.shape
    tiles = width // LANES
    tile = lax.axis_index("tile")
    count_tiles = lax.axis_size("tile")
    core = lax.axis_index("member") % 2
    first = tile * rows
    even = tile % 2 == 0
    per = members * (2 * FIELDS + 2 * NLAYER)
    total_rows = rows + 2 * PAD
    zero = jnp.zeros((total_rows, LANES), jnp.float32)
    inside = slice(PAD, PAD + rows)

    for mf in range(members * FIELDS):
        for i in range(tiles):
            s0[mf, i + 1, inside, :] = state[mf // FIELDS, mf % FIELDS, :, i * LANES : (i + 1) * LANES]
        for buffer in (s0, s1):
            buffer[mf, 0, :, :] = zero
            buffer[mf, tiles + 1, :, :] = zero
    for mc in range(members * 2 * NLAYER):
        for i in range(tiles):
            vs[mc, i, inside, :] = vel[mc // (2 * NLAYER), mc % (2 * NLAYER), :, i * LANES : (i + 1) * LANES]

    def edge(source, row, vrow):
        for i in range(tiles):
            for mf in range(members * FIELDS):
                at = i * per + mf * 2
                s0[mf, i + 1, row : row + 2, :] = source[at : at + 2, :]
            for mc in range(members * 2 * NLAYER):
                at = i * per + members * FIELDS * 2 + mc
                vs[mc, i, vrow : vrow + 1, :] = source[at : at + 1, :]

    @pl.when(even)
    def _():
        edge(from_a, PAD + rows, PAD + rows)
        edge(from_b, PAD - 2, PAD - 1)

    @pl.when(jnp.logical_not(even))
    def _():
        edge(from_a, PAD - 2, PAD - 1)
        edge(from_b, PAD + rows, PAD + rows)

    lane = lane_index()
    at_left = lane == 0
    at_right = lane == LANES - 1

    def advance(source, f, i, r, coef):
        centre = source[f, i + 1, r : r + 8, :]
        up = source[f, i + 1, r - 1 : r + 7, :]
        down = source[f, i + 1, r + 1 : r + 9, :]
        before = source[f, i, r : r + 8, :]
        after = source[f, i + 2, r : r + 8, :]
        left = pltpu.roll(jnp.where(at_right, before, centre), 1, 1)
        right = pltpu.roll(jnp.where(at_left, after, centre), LANES - 1, 1)
        return stencil(coef, centre, up, down, left, right)

    def first_step(t, carry):
        ml, i = t // tiles, t % tiles
        for r in range(PAD - 1, PAD + rows + 1, 8):
            coef = coefficients(vs[2 * ml, i, r : r + 8, :], vs[2 * ml + 1, i, r : r + 8, :])
            for k in range(KINDS):
                s1[ml * KINDS + k, i + 1, r : r + 8, :] = advance(s0, ml * KINDS + k, i, r, coef)
        return carry

    lax.fori_loop(0, members * NLAYER * tiles, first_step, 0)

    @pl.when(tile == 0)
    def _():
        s1[:, :, PAD - 1 : PAD, :] = jnp.zeros((members * FIELDS, tiles + 2, 1, LANES), jnp.float32)

    @pl.when(tile == count_tiles - 1)
    def _():
        s1[:, :, PAD + rows : PAD + rows + 1, :] = jnp.zeros(
            (members * FIELDS, tiles + 2, 1, LANES), jnp.float32
        )

    def second_step(t, carry):
        m, i = t // tiles, t % tiles
        lanes = pl.ds(pl.multiple_of(i * LANES, LANES), LANES)
        for r in range(PAD, PAD + rows, 8):
            coefs = []
            for l in range(NLAYER):
                mc = (m * NLAYER + l) * 2
                coefs.append(coefficients(vs[mc, i, r : r + 8, :], vs[mc + 1, i, r : r + 8, :]))
            bins = band[r - PAD : r - PAD + 8, lanes]
            for k in range(KINDS):
                upper = m * FIELDS + k
                lower = upper + KINDS
                a = advance(s1, upper, i, r, coefs[0])
                b = advance(s1, lower, i, r, coefs[1])
                if k > 0:
                    rate = jnp.full((8, LANES), table[0, k - 1], jnp.float32)
                    for level in range(1, table.shape[0]):
                        rate = jnp.where(bins == level, table[level, k - 1], rate)
                    settled = rate * a
                    a, b = a - settled, b + settled - DEPOSIT * rate * b
                for f, value in ((k, a), (k + KINDS, b)):
                    padded[m * FIELDS + f, i, r : r + 8, :] = value
                    out[m, f, r - PAD : r - PAD + 8, lanes] = value
        return carry

    lax.fori_loop(0, members * tiles, second_step, 0)

    for mf in range(members * FIELDS):
        for i in range(tiles):
            padded[mf, i, :PAD, :] = zero[:PAD]
            padded[mf, i, PAD + rows :, :] = zero[:PAD]

    base = tiles * per
    blocks = []
    for n in range(NEAR_BLOCKS):
        block = from_a[base + 8 * n : base + 8 * n + 8, :]
        for near in nears:
            block = block + near[8 * n : 8 * n + 8, :]
        blocks.append(block)

    def step(up, centre, down, coef):
        return stencil(
            coef, centre, up, down, pltpu.roll(centre, 1, 1), pltpu.roll(centre, LANES - 1, 1)
        )

    coefs = [coefficients(blocks[5 + i], blocks[8 + i]) for i in range(3)]
    once = [step(blocks[i], blocks[i + 1], blocks[i + 2], coefs[i]) for i in range(3)]
    value = step(once[0], once[1], once[2], coefs[1])
    bins = jnp.broadcast_to(blocks[11][:1], (8, LANES))
    kinds = spread(kind, GROUP)
    rate = jnp.zeros((8, LANES), jnp.float32)
    for level in range(table.shape[0]):
        here = jnp.abs(bins - level) < 0.5
        for k in range(NCLASS):
            rate = jnp.where(here & (kinds == k + 1), table[level, k], rate)
    bottom = row_index() % 2 == 1
    above = pltpu.roll(value, 1, 0)
    settled = jnp.where(
        bottom, value + rate * above - DEPOSIT * rate * value, value - rate * value
    )
    settled = jnp.where(spread(layer, GROUP) == 0, settled, pltpu.roll(settled, 7, 0))
    squeeze = (
        lax.broadcasted_iota(jnp.int32, (LANES, LANES), 0)
        == lax.broadcasted_iota(jnp.int32, (LANES, LANES), 1) * GROUP + 2
    ).astype(jnp.float32)
    seen = jnp.dot(settled, squeeze, precision=EXACT, preferred_element_type=jnp.float32)
    obs_out[...] = jnp.zeros((8, LANES), jnp.float32)
    for m in range(members):
        obs_out[m : m + 1, :] = seen[2 * m : 2 * m + 1]

    size = cap * WINDOW_HEIGHT
    count = find_slots(lat, slots, first, rows, cap)
    for s in range(cap):
        sel[s * 4 : s * 4 + 4, :] = (lane[:4] == slots[s]).astype(jnp.float32)
    send[members * KINDS * size :, :] = obs_out[...]

    def cut(layer_of_own):
        def one(s, carry):
            row, block, after, shift = window(lat, lon, slots[s], first, rows, tiles)
            here = lane >= shift
            for l, target in ((layer_of_own, own), (1 - layer_of_own, send)):
                for m in range(members):
                    for k in range(KINDS):
                        f = m * FIELDS + l * KINDS + k
                        both = jnp.where(
                            here, padded[f, block, pl.ds(row, 8), :], padded[f, after, pl.ds(row, 8), :]
                        )
                        patch = pltpu.roll(both, (LANES - shift) % LANES, 1)
                        target[pl.ds((m * KINDS + k) * size + s * 4, 4), :] = patch[:4]
            return carry

        lax.fori_loop(0, count, one, 0)

    for c in range(2):
        pl.when(core == c)(functools.partial(cut, c))


def pair_kernel(cap, members, own, got, obs, sel, msg):
    size = cap * WINDOW_HEIGHT
    part = KINDS * size
    seen = obs[:members, :]
    theirs = got[members * part : members * part + members, :]
    mean = (jnp.sum(seen, axis=0, keepdims=True) + jnp.sum(theirs, axis=0, keepdims=True)) / (2 * members)
    sources = [(own, m, seen[m : m + 1]) for m in range(members)]
    sources += [(got, m, theirs[m : m + 1]) for m in range(members)]
    weight = [jnp.sum(sel[...] * (o - mean), axis=1, keepdims=True) for _, _, o in sources]
    for k in range(KINDS):
        cross = jnp.zeros((size, LANES), jnp.float32)
        total = jnp.zeros((size, LANES), jnp.float32)
        for (ref, m, _), o in zip(sources, weight):
            patch = ref[m * part + k * size : m * part + (k + 1) * size, :]
            cross = cross + patch * o
            total = total + patch
        msg[k * size : (k + 1) * size, :] = cross
        msg[part + k * size : part + (k + 1) * size, :] = total
    msg[2 * part :, :] = jnp.zeros((8, LANES), jnp.float32)
    msg[2 * part : 2 * part + members, :] = seen
    msg[2 * part + members : 2 * part + 2 * members, :] = theirs


def merge_kernel(cap, members, chips, value, error, perturb, obs, sel, *rest):
    msgs, (gain, weights, everyone) = rest[:chips], rest[chips:]
    size = cap * WINDOW_HEIGHT
    part = KINDS * size
    both = 2 * members
    number = chips * both
    observations = value.shape[0]
    means = []
    for c, msg in enumerate(msgs):
        seen = msg[2 * part : 2 * part + both, :]
        everyone[c * both : (c + 1) * both, :] = seen
        means.append(jnp.sum(seen, axis=0, keepdims=True) / both)
    mean = functools.reduce(jnp.add, means) / chips
    shifts = [jnp.sum(sel[...] * (own - mean), axis=1, keepdims=True) for own in means]
    row = (row_index(size) % WINDOW_HEIGHT).astype(jnp.float32)
    column = lane_index(size).astype(jnp.float32)
    row = (row + 0.5 - WINDOW_HEIGHT / 2) / (WINDOW_HEIGHT / 2)
    column = (column + 0.5 - WINDOW_WIDTH / 2) / (WINDOW_WIDTH / 2)
    taper = (1.0 - row * row) * (1.0 - column * column) / (number - 1)
    for k in range(KINDS):
        cross = jnp.zeros((size, LANES), jnp.float32)
        for msg, shift in zip(msgs, shifts):
            cross = cross + msg[k * size : (k + 1) * size, :]
            cross = cross + shift * msg[part + k * size : part + (k + 1) * size, :]
        gain[k * size : (k + 1) * size, :] = taper * cross
    gain[part:, :] = jnp.zeros((8, LANES), jnp.float32)

    anomaly = everyone[...] - mean
    over = (((0,), (0,)), ((), ()))
    cov = lax.dot_general(anomaly, anomaly, over, precision=EXACT, preferred_element_type=jnp.float32)
    row16 = row_index(observations)
    lane16 = lane_index(observations)
    errors = spread(error, 1)
    innovation = spread(value, 1)[:members] - obs[:members, :]
    noise = jnp.concatenate(
        [perturb[...], jnp.zeros((members, LANES - observations), jnp.float32)], axis=1
    )
    innovation = innovation + jnp.sqrt(errors[:members]) * noise
    place = (lane_index(members) == row_index(members) + observations).astype(jnp.float32)
    sides = lax.dot_general(innovation, place, over, precision=EXACT, preferred_element_type=jnp.float32)
    system = jnp.where(lane16 < observations, cov[:observations] / (number - 1), sides[:observations])
    system = system + jnp.where(lane16 == row16, jnp.broadcast_to(errors[:1], row16.shape), 0.0)
    for k in range(observations):
        pivot = system[k : k + 1, :] / system[k : k + 1, k : k + 1]
        system = jnp.where(row16 == k, pivot, system - system[:, k : k + 1] * pivot)
    for m in range(members):
        weights[m, :, :] = jnp.broadcast_to(
            system[:, observations + m : observations + m + 1], (observations, LANES)
        )


def apply_kernel(cap, lat, lon, field, mine, theirs, weights, out, work, slots):
    members, _, rows, width = field.shape
    tiles = width // LANES
    size = cap * WINDOW_HEIGHT
    first = lax.axis_index("tile") * rows
    core = lax.axis_index("member") % 2
    for mf in range(members * FIELDS):
        for i in range(tiles):
            work[mf, i, PAD : PAD + rows, :] = field[
                mf // FIELDS, mf % FIELDS, :, i * LANES : (i + 1) * LANES
            ]
    count = find_slots(lat, slots, first, rows, cap)
    lane = lane_index()
    patch_row = row_index() < WINDOW_HEIGHT

    def add(layer_of_own):
        def one(s, carry):
            j = slots[s]
            row, block, after, shift = window(lat, lon, j, first, rows, tiles)
            here = patch_row & (lane >= shift)
            there = patch_row & (lane < shift)
            w = [weights[m, pl.ds(j, 1), :] for m in range(members)]
            for l, source in ((layer_of_own, mine), (1 - layer_of_own, theirs)):
                for k in range(KINDS):
                    gain = pltpu.roll(source[pl.ds(k * size + s * 4, 8), :], shift, 1)
                    near = jnp.where(here, gain, 0.0)
                    far = jnp.where(there, gain, 0.0)
                    for m in range(members):
                        f = m * FIELDS + l * KINDS + k
                        work[f, block, pl.ds(row, 8), :] += near * w[m]
                        work[f, after, pl.ds(row, 8), :] += far * w[m]
            return carry

        lax.fori_loop(0, count, one, 0)

    for c in range(2):
        pl.when(core == c)(functools.partial(add, c))
    for mf in range(members * FIELDS):
        for i in range(tiles):
            out[mf // FIELDS, mf % FIELDS, :, i * LANES : (i + 1) * LANES] = work[
                mf, i, PAD : PAD + rows, :
            ]


def partner(size, k):
    if size & (size - 1) == 0:
        return [(i, i ^ k) for i in range(size)]
    return [(i, (i + k) % size) for i in range(size)]


def body(state, vel, band, table, lat, lon, layer, kind, value, error, perturb):
    members, _, rows, width = state.shape
    tiles = width // LANES
    row_tiles = lax.axis_size("tile")
    devices = lax.axis_size("member")
    chips = devices // 2
    observations = lat.shape[0]
    per = members * (2 * FIELDS + 2 * NLAYER)
    edge = tiles * per
    near_rows = NEAR_BLOCKS * 8
    out_a, out_b, near = call(
        pack_kernel,
        "pack_edges",
        [SMEM] * 3 + [VMEM] * 3,
        [(edge + near_rows, LANES), (edge, LANES), (near_rows, LANES)],
    )(lat, lon, kind, state, vel, band)
    pairs_a = [(i, i + 1) for i in range(0, row_tiles - 1, 2)]
    pairs_b = [(i, i + 1) for i in range(1, row_tiles - 1, 2)]
    from_a = lax.ppermute(out_a, "tile", pairs_a + [(j, i) for i, j in pairs_a])
    from_b = lax.ppermute(out_b, "tile", pairs_b + [(j, i) for i, j in pairs_b])
    nears = [near] + [lax.ppermute(near, "tile", partner(row_tiles, k)) for k in range(2, row_tiles)]

    cap = observations
    size = cap * WINDOW_HEIGHT
    part = KINDS * size
    padded_rows = rows + 2 * PAD
    field, own, send, obs, sel = call(
        functools.partial(forecast_kernel, cap, len(nears) - 1),
        "forecast",
        [SMEM] * 5 + [VMEM] * (5 + len(nears)),
        [
            state.shape,
            (members * part, LANES),
            (members * part + 8, LANES),
            (8, LANES),
            (size, LANES),
        ],
        [
            pltpu.VMEM((members * FIELDS, tiles + 2, padded_rows, LANES), jnp.float32),
            pltpu.VMEM((members * FIELDS, tiles + 2, padded_rows, LANES), jnp.float32),
            pltpu.VMEM((members * 2 * NLAYER, tiles, padded_rows, LANES), jnp.float32),
            pltpu.VMEM((members * FIELDS, tiles, padded_rows, LANES), jnp.float32),
            pltpu.SMEM((cap + 1,), jnp.int32),
        ],
    )(lat, lon, layer, kind, table, state, vel, band, from_a, from_b, *nears)
    got = lax.ppermute(send, "member", [(i, i ^ 1) for i in range(devices)])
    (msg,) = call(
        functools.partial(pair_kernel, cap, members),
        "pair_moments",
        [VMEM] * 4,
        [(2 * part + 8, LANES)],
    )(own, got, obs, sel)
    msgs = [msg] + [lax.ppermute(msg, "member", partner(devices, 2 * k)) for k in range(1, chips)]
    mine, weights = call(
        functools.partial(merge_kernel, cap, members, chips),
        "merge_moments",
        [SMEM] * 2 + [VMEM] * (3 + chips),
        [(part + 8, LANES), (members, observations, LANES)],
        [pltpu.VMEM((chips * 2 * members, LANES), jnp.float32)],
    )(value, error, perturb, obs, sel, *msgs)
    theirs = lax.ppermute(mine, "member", [(i, i ^ 1) for i in range(devices)])
    (analysed,) = call(
        functools.partial(apply_kernel, cap),
        "apply_increments",
        [SMEM] * 2 + [VMEM] * 4,
        [state.shape],
        [
            pltpu.VMEM((members * FIELDS, tiles, padded_rows, LANES), jnp.float32),
            pltpu.SMEM((cap + 1,), jnp.int32),
        ],
    )(lat, lon, field, mine, theirs, weights)
    return analysed


def solution(mesh):
    placed = (
        P("member", None, "tile", None),
        P("member", None, "tile", None),
        P("tile", None),
        P(),
        P(),
        P(),
        P(),
        P(),
        P(),
        P(),
        P("member", None),
    )
    return jax.shard_map(
        body, mesh=mesh, in_specs=placed, out_specs=P("member", None, "tile", None), check_vma=False
    )
```

```python
import functools

import jax
import jax.numpy as jnp
from jax import lax
from jax.experimental import pallas as pl
from jax.experimental.pallas import tpu as pltpu
from jax.sharding import PartitionSpec as P

NLAYER = 2
NCLASS = 4
KINDS = NCLASS + 1
FIELDS = NLAYER * KINDS
WINDOW_HEIGHT = 4
WINDOW_WIDTH = 128
DIFFUSION = 0.08
DEPOSIT = 0.5
CAP = 16

LANES = 128
PAD = 8
GROUP = 8
NEAR_ROWS = 48
EXACT = lax.Precision.HIGHEST
MIB = 1024 * 1024

SMEM = pl.BlockSpec(memory_space=pltpu.SMEM)
VMEM = pl.BlockSpec(memory_space=pltpu.VMEM)
HBM = pl.BlockSpec(memory_space=pltpu.HBM)


def call(kernel, name, in_specs, outs, scratch=(), flops=1000, aliases=None, limit=40):
    return pl.pallas_call(
        kernel,
        name=name,
        in_specs=in_specs,
        out_specs=[VMEM] * len(outs),
        out_shape=[jax.ShapeDtypeStruct(shape, jnp.float32) for shape in outs],
        scratch_shapes=list(scratch),
        input_output_aliases=aliases or {},
        compiler_params=pltpu.CompilerParams(vmem_limit_bytes=limit * MIB),
        cost_estimate=pl.CostEstimate(flops=flops, bytes_accessed=1000, transcendentals=0),
    )


def held(*arrays):
    return [pltpu.with_memory_space_constraint(array, pltpu.HBM) for array in arrays]


def lane_index(rows=8):
    return lax.broadcasted_iota(jnp.int32, (rows, LANES), 1)


def row_index(rows=8):
    return lax.broadcasted_iota(jnp.int32, (rows, LANES), 0)


def spread(ref, group, rows=8):
    index = lane_index(rows) // group
    total = jnp.zeros((rows, LANES), ref.dtype)
    for j in range(ref.shape[0]):
        total = jnp.where(index == j, ref[j], total)
    return total


def find_slots(lat, slots, first, rows, cap):
    for s in range(cap + 1):
        slots[s] = 0
    count = jnp.int32(0)
    for j in range(lat.shape[0]):
        start = lat[j] - WINDOW_HEIGHT // 2 - first
        slots[jnp.minimum(count, cap)] = j
        count = count + ((start < rows) & (start + WINDOW_HEIGHT > 0)).astype(jnp.int32)
    return jnp.minimum(count, cap)


def window(lat, lon, j, first, rows, tiles):
    row = jnp.clip(lat[j] - WINDOW_HEIGHT // 2 - first, -WINDOW_HEIGHT, rows) + PAD
    left = lon[j] - WINDOW_WIDTH // 2
    block = left // LANES
    return row, block, jnp.minimum(block + 1, tiles - 1), left % LANES


def coefficients(u, w):
    return (
        (1.0 - 4.0 * DIFFUSION) - (jnp.abs(u) + jnp.abs(w)),
        jnp.maximum(u, 0.0) + DIFFUSION,
        DIFFUSION - jnp.minimum(u, 0.0),
        jnp.maximum(w, 0.0) + DIFFUSION,
        DIFFUSION - jnp.minimum(w, 0.0),
    )


def stencil(coef, centre, up, down, left, right):
    return (coef[0] * centre + coef[1] * up) + (coef[2] * down + coef[3] * left) + coef[4] * right


def choose(values, pick):
    total = jnp.zeros((values.shape[0], LANES), jnp.float32)
    for _ in range(3):
        part = values.astype(jnp.bfloat16)
        total = total + jnp.dot(part, pick, preferred_element_type=jnp.float32)
        values = values - part.astype(jnp.float32)
    return total


def lane_tiles(source, target, members, tiles, each, rows, shift):
    return [
        (
            source.at[m, :, :, pl.ds(i * LANES, LANES)],
            target.at[pl.ds(m * each, each), i + shift, pl.ds(PAD, rows), :],
        )
        for m in range(members)
        for i in range(tiles)
    ]


def start_copies(moves, sems):
    copies = [pltpu.make_async_copy(src, dst, sems.at[n]) for n, (src, dst) in enumerate(moves)]
    for copy in copies:
        copy.start()
    return copies


def pack_kernel(lat_hbm, lon_hbm, kind_hbm, state_hbm, vel_hbm, band_hbm, out_a, out_b, near, s0, vs, bs, lat, lon, kind, sems):
    members, _, rows, width = state_hbm.shape
    tiles = width // LANES
    fields, parts = members * FIELDS, members * 2 * NLAYER
    moves = lane_tiles(state_hbm, s0, members, tiles, FIELDS, rows, 0)
    moves += lane_tiles(vel_hbm, vs, members, tiles, 2 * NLAYER, rows, 0)
    moves += [(band_hbm.at[:, pl.ds(i * LANES, LANES)], bs.at[i, pl.ds(PAD, rows), :]) for i in range(tiles)]
    moves += [(lat_hbm, lat), (lon_hbm, lon), (kind_hbm, kind)]
    copies = start_copies(moves, sems)
    tile = lax.axis_index("tile")
    even = tile % 2 == 0
    first = tile * rows
    zero = jnp.zeros((PAD, LANES), jnp.float32)
    for ref in (s0, vs, bs):
        for n in range(ref.shape[0]) if ref is not bs else (None,):
            for i in range(tiles):
                lead = (i,) if n is None else (n, i)
                ref[lead + (slice(0, PAD),)] = zero.astype(ref.dtype)
                ref[lead + (slice(PAD + rows, None),)] = zero.astype(ref.dtype)
    for copy in copies:
        copy.wait()

    def edge(out, q_first, v_at):
        for i in range(tiles):
            for c in range(parts):
                to = NEAR_ROWS + i * parts + c
                out[to : to + 1, :] = vs[c, i, v_at : v_at + 1, :]
            for f in range(fields):
                to = NEAR_ROWS + tiles * parts + (i * fields + f) * 2
                out[to : to + 2, :] = s0[f, i, q_first : q_first + 2, :]

    top, bottom = PAD, PAD + rows

    @pl.when(even)
    def _():
        edge(out_a, bottom - 2, bottom - 1)
        edge(out_b, top, top)

    @pl.when(jnp.logical_not(even))
    def _():
        edge(out_a, top, top)
        edge(out_b, bottom - 2, bottom - 1)

    lane = lane_index()
    row = row_index()
    blank = jnp.zeros((8, LANES), jnp.float32)
    pairs = members * NLAYER
    qs, us, ws, bins = [blank] * pairs, [blank] * pairs, [blank] * pairs, blank
    for j in range(lat.shape[0]):
        start = jnp.clip(lat[j] - 2 - first, -PAD, rows) + PAD
        left = lon[j] - 2
        block, shift = left // LANES, left % LANES
        after = jnp.minimum(block + 1, tiles - 1)
        turn = (GROUP * j - shift + LANES) % LANES
        here = lane >= shift
        mine = (lane // GROUP) == j

        def fetch(ref, old, *lead):
            both = jnp.where(
                here, ref[lead + (block, pl.ds(start, 8))], ref[lead + (after, pl.ds(start, 8))]
            )
            return jnp.where(mine, pltpu.roll(both.astype(jnp.float32), turn, 1), old)

        for m in range(members):
            for l in range(NLAYER):
                s = m * NLAYER + l
                qs[s] = fetch(s0, qs[s], m * FIELDS + l * KINDS + kind[j])
                us[s] = fetch(vs, us[s], 2 * s)
                ws[s] = fetch(vs, ws[s], 2 * s + 1)
        bins = fetch(bs, bins)

    blocks = [jnp.where(row < 5, q, pltpu.roll(u, 4, 0)) for q, u in zip(qs, us)]
    for m in range(members):
        w = jnp.where(row < 4, ws[2 * m], pltpu.roll(ws[2 * m + 1], 4, 0))
        blocks.append(jnp.where(row == 0, pltpu.roll(bins, 6, 0), w))
    for n, block in enumerate(blocks):
        for out in (near, out_a, out_b):
            out[8 * n : 8 * n + 8, :] = block


def combine_kernel(near, from_a, _, out):
    out[...] = near[...] + from_a[:NEAR_ROWS, :]


def advance(source, f, i, r, coef, lane):
    centre = source[f, i + 1, r : r + 8, :]
    up = source[f, i + 1, r - 1 : r + 7, :]
    down = source[f, i + 1, r + 1 : r + 9, :]
    left, right = sides_of(source[f, i, r : r + 8, :], centre, source[f, i + 2, r : r + 8, :], lane)
    return stencil(coef, centre, up, down, left, right)


def sides_of(before, centre, after, lane):
    left = pltpu.roll(jnp.where(lane == LANES - 1, before, centre), 1, 1)
    right = pltpu.roll(jnp.where(lane == 0, after, centre), LANES - 1, 1)
    return left, right


def settle(a, b, bins, table, k):
    if k == 0:
        return a, b
    rate = jnp.full(a.shape, table[0, k - 1], jnp.float32)
    for level in range(1, table.shape[0]):
        rate = jnp.where(bins == level, table[level, k - 1], rate)
    settled = rate * a
    return a - settled, b + settled - DEPOSIT * rate * b


def interior_kernel(table_hbm, state, vel, band_hbm, padded, own_edge, once_edge, vel_edge, bin_edge, s0, s1, vs, band, table, sems):
    members, _, rows, width = state.shape
    tiles = width // LANES
    fields, parts = members * FIELDS, members * 2 * NLAYER
    moves = lane_tiles(vel, vs, members, tiles, 2 * NLAYER, rows, 0)
    moves += lane_tiles(state, s0, members, tiles, FIELDS, rows, 1)
    moves += [(band_hbm, band), (table_hbm, table)]
    copies = start_copies(moves, sems)
    zero = jnp.zeros((rows + 2 * PAD, LANES), jnp.float32)
    lane = lane_index()
    for f in range(fields):
        for buffer in (s0, s1):
            buffer[f, 0, :, :] = zero
            buffer[f, tiles + 1, :, :] = zero
    for copy in copies:
        copy.wait()

    def first_step(t, carry):
        ml, i = t // tiles, t % tiles
        for r in range(PAD, PAD + rows, 8):
            coef = coefficients(vs[2 * ml, i, r : r + 8, :], vs[2 * ml + 1, i, r : r + 8, :])
            for k in range(KINDS):
                s1[ml * KINDS + k, i + 1, r : r + 8, :] = advance(s0, ml * KINDS + k, i, r, coef, lane)
        return carry

    for t in range(members * NLAYER * tiles):
        first_step(t, 0)

    def second_step(t, carry):
        m, i = t // tiles, t % tiles
        lanes = pl.ds(i * LANES, LANES)
        for r in range(PAD, PAD + rows, 8):
            coefs = []
            for l in range(NLAYER):
                mc = (m * NLAYER + l) * 2
                coefs.append(coefficients(vs[mc, i, r : r + 8, :], vs[mc + 1, i, r : r + 8, :]))
            bins = band[r - PAD : r - PAD + 8, lanes]
            for k in range(KINDS):
                upper = m * FIELDS + k
                lower = upper + KINDS
                a = advance(s1, upper, i, r, coefs[0], lane)
                b = advance(s1, lower, i, r, coefs[1], lane)
                a, b = settle(a, b, bins, table, k)
                padded[upper, i, r : r + 8, :] = a
                padded[lower, i, r : r + 8, :] = b
        return carry

    for t in range(members * tiles):
        second_step(t, 0)

    top, bottom = PAD, PAD + rows
    half = row_index() < 4

    def halves(ref, lead, low, high):
        return jnp.where(half, ref[lead + (slice(low, low + 8), slice(None))], ref[lead + (slice(high - 4, high + 4), slice(None))])

    for i in range(tiles):
        for f in range(fields):
            padded[f, i, :PAD, :] = zero[:PAD]
            padded[f, i, PAD + rows :, :] = zero[:PAD]
            own_edge[f, i, :, :] = halves(s0, (f, i + 1), top - 2, bottom - 2)
            once_edge[f, i, :, :] = halves(s1, (f, i + 1), top - 1, bottom - 3)
        for c in range(parts):
            vel_edge[0, c, i, :, :] = halves(vs, (c, i), top - 2, bottom - 2)
            vel_edge[1, c, i, :, :] = halves(vs, (c, i), top - 1, bottom - 3)
        upper = band[0:8, i * LANES : (i + 1) * LANES].astype(jnp.float32)
        lower = band[rows - 8 : rows, i * LANES : (i + 1) * LANES].astype(jnp.float32)
        bin_edge[i, :, :] = jnp.where(half, pltpu.roll(upper, 1, 0), pltpu.roll(lower, 7, 0))


def observe_kernel(members, layer, kind, table, *rest):
    parts, out = rest[:-1], rest[-1]
    pairs = members * NLAYER
    blocks = []
    for n in range(pairs + members):
        block = parts[0][8 * n : 8 * n + 8, :]
        for more in parts[1:]:
            block = block + more[8 * n : 8 * n + 8, :]
        blocks.append(block)
    bins = jnp.broadcast_to(blocks[pairs][:1], (8, LANES))
    kinds = spread(kind, GROUP)
    layers = spread(layer, GROUP)
    rate = jnp.zeros((8, LANES), jnp.float32)
    for level in range(table.shape[0]):
        here = jnp.abs(bins - level) < 0.5
        for k in range(NCLASS):
            rate = jnp.where(here & (kinds == k + 1), table[level, k], rate)
    row = row_index()

    def step(q, coef):
        return stencil(
            coef,
            q,
            pltpu.roll(q, 1, 0),
            pltpu.roll(q, 7, 0),
            pltpu.roll(q, 1, 1),
            pltpu.roll(q, LANES - 1, 1),
        )

    seen = jnp.zeros((8, LANES), jnp.float32)
    for m in range(members):
        values = []
        for l in range(NLAYER):
            q = blocks[m * NLAYER + l]
            u = pltpu.roll(q, 4, 0)
            w = blocks[pairs + m]
            coef = coefficients(u, w if l == 0 else pltpu.roll(w, 4, 0))
            values.append(step(step(q, coef), coef))
        a, b = values
        settled = rate * a
        value = jnp.where(layers == 0, a - settled, b + settled - DEPOSIT * rate * b)
        seen = jnp.where(row == m, pltpu.roll(value, (m - 2) % 8, 0), seen)
    squeeze = (
        lax.broadcasted_iota(jnp.int32, (LANES, LANES), 0)
        == lax.broadcasted_iota(jnp.int32, (LANES, LANES), 1) * GROUP + 2
    ).astype(jnp.bfloat16)
    out[...] = choose(seen, squeeze)


def join_kernel(members, obs, got, out):
    out[...] = jnp.where(row_index() < members, obs[...], pltpu.roll(got[...], members, 0))


def edge_kernel(table, own_edge, once_edge, vel_edge, bin_edge, from_a, from_b, inner, near, padded, e0, e1, up, down):
    fields, tiles, padded_rows, _ = padded.shape
    rows = padded_rows - 2 * PAD
    members = fields // FIELDS
    parts = members * 2 * NLAYER
    tile = lax.axis_index("tile")
    count_tiles = lax.axis_size("tile")
    even = tile % 2 == 0
    sent = from_a.shape[0]

    @pl.when(even)
    def _():
        down[:sent, :] = from_a[...]
        up[:sent, :] = from_b[...]

    @pl.when(jnp.logical_not(even))
    def _():
        up[:sent, :] = from_a[...]
        down[:sent, :] = from_b[...]

    lane = lane_index()
    row = row_index()
    zero = jnp.zeros((8, LANES), jnp.float32)
    v_base = NEAR_ROWS
    q_base = NEAR_ROWS + tiles * parts
    for f in range(fields):
        for buffer in (e0, e1):
            buffer[f, 0, :, :] = zero
            buffer[f, tiles + 1, :, :] = zero

    def gather(i, carry):
        for f in range(fields):
            at = q_base + (i * fields + f) * 2
            q = jnp.where(row < 2, up[pl.ds(at, 8), :], own_edge[f, i, :, :])
            e0[f, i + 1, :, :] = jnp.where(row > 5, down[pl.ds(at - 6, 8), :], q)
        return carry

    for i in range(tiles):
        gather(i, 0)
    outside = ((row == 0) & (tile == 0)) | ((row == 7) & (tile == count_tiles - 1))

    def first_step(t, carry):
        ml, i = t // tiles, t % tiles
        flow = []
        for c in range(2):
            at = v_base + i * parts + 2 * ml + c
            v = jnp.where(row == 1, up[pl.ds(at - 1, 8), :], vel_edge[0, 2 * ml + c, i, :, :])
            flow.append(jnp.where(row == 6, down[pl.ds(at - 6, 8), :], v))
        coef = coefficients(*flow)
        for k in range(KINDS):
            f = ml * KINDS + k
            centre = e0[f, i + 1, :, :]
            left, right = sides_of(e0[f, i, :, :], centre, e0[f, i + 2, :, :], lane)
            q = stencil(coef, centre, pltpu.roll(centre, 1, 0), pltpu.roll(centre, 7, 0), left, right)
            q = jnp.where(row < 2, pltpu.roll(q, 7, 0), jnp.where(row > 5, pltpu.roll(q, 1, 0), once_edge[f, i, :, :]))
            e1[f, i + 1, :, :] = jnp.where(outside, 0.0, q)
        return carry

    for t in range(members * NLAYER * tiles):
        first_step(t, 0)

    def second_step(t, carry):
        m, i = t // tiles, t % tiles
        bins = bin_edge[i, :, :].astype(jnp.int32)
        values = []
        for l in range(NLAYER):
            mc = (m * NLAYER + l) * 2
            coef = coefficients(vel_edge[1, mc, i, :, :], vel_edge[1, mc + 1, i, :, :])
            for k in range(KINDS):
                f = m * FIELDS + l * KINDS + k
                centre = e1[f, i + 1, :, :]
                left, right = sides_of(e1[f, i, :, :], centre, e1[f, i + 2, :, :], lane)
                values.append(
                    stencil(coef, centre, pltpu.roll(centre, 1, 0), pltpu.roll(centre, 7, 0), left, right)
                )
        for k in range(KINDS):
            for l, q in enumerate(settle(values[k], values[KINDS + k], bins, table, k)):
                f = m * FIELDS + l * KINDS + k
                padded[f, i, PAD : PAD + 2, :] = q[1:3]
                padded[f, i, PAD + rows - 2 : PAD + rows, :] = q[5:7]
        return carry

    for t in range(members * tiles):
        second_step(t, 0)


def cut_kernel(cap, lat, lon, padded, _, own, send, sel, slots):
    fields, tiles, padded_rows, _ = padded.shape
    rows = padded_rows - 2 * PAD
    members = fields // FIELDS
    core = lax.axis_index("member") % 2
    first = lax.axis_index("tile") * rows
    lane = lane_index()
    size = cap * WINDOW_HEIGHT
    count = find_slots(lat, slots, first, rows, cap)
    for s in range(cap):
        sel[s * 4 : s * 4 + 4, :] = (lane[:4] == slots[s]).astype(jnp.float32)

    def cut(layer_of_own):
        def one(s, carry):
            row, block, after, shift = window(lat, lon, slots[s], first, rows, tiles)
            here = lane >= shift
            for l, target in ((layer_of_own, own), (1 - layer_of_own, send)):
                for m in range(members):
                    for k in range(KINDS):
                        f = m * FIELDS + l * KINDS + k
                        both = jnp.where(
                            here, padded[f, block, pl.ds(row, 8), :], padded[f, after, pl.ds(row, 8), :]
                        )
                        patch = pltpu.roll(both, (LANES - shift) % LANES, 1)
                        target[pl.ds((m * KINDS + k) * size + s * 4, 4), :] = patch[:4]
            return carry

        lax.fori_loop(0, count, one, 0)

    for c in range(2):
        pl.when(core == c)(functools.partial(cut, c))


def moment_kernel(cap, members, chips, own, got, sel, *rest):
    seens, (cross, everyone) = rest[:chips], rest[chips:]
    size = cap * WINDOW_HEIGHT
    part = KINDS * size
    both = 2 * members
    for c, seen in enumerate(seens):
        everyone[c * both : (c + 1) * both, :] = seen[:both, :]
    mean = jnp.sum(everyone[...], axis=0, keepdims=True) / (chips * both)
    sources = [(own, m, m) for m in range(members)] + [(got, m, members + m) for m in range(members)]
    weight = [
        jnp.sum(sel[...] * (everyone[o : o + 1, :] - mean), axis=1, keepdims=True) for _, _, o in sources
    ]
    for k in range(KINDS):
        total = jnp.zeros((size, LANES), jnp.float32)
        for (ref, m, _), o in zip(sources, weight):
            total = total + ref[m * part + k * size : m * part + (k + 1) * size, :] * o
        cross[k * size : (k + 1) * size, :] = total


def weight_kernel(value, error, perturb, everyone_ref, weights):
    members, observations = perturb.shape
    everyone = everyone_ref[...]
    number = everyone.shape[0]
    anomaly = everyone - jnp.sum(everyone, axis=0, keepdims=True) / number
    over = (((0,), (0,)), ((), ()))
    cov = lax.dot_general(anomaly, anomaly, over, precision=EXACT, preferred_element_type=jnp.float32)
    row16 = row_index(observations)
    lane16 = lane_index(observations)
    errors = spread(error, 1)
    innovation = spread(value, 1)[:members] - everyone[:members]
    noise = jnp.concatenate(
        [perturb[...], jnp.zeros((members, LANES - observations), jnp.float32)], axis=1
    )
    innovation = innovation + jnp.sqrt(errors[:members]) * noise
    place = (lane_index(members) == row_index(members) + observations).astype(jnp.float32)
    sides = lax.dot_general(innovation, place, over, precision=EXACT, preferred_element_type=jnp.float32)
    system = jnp.where(lane16 < observations, cov[:observations] / (number - 1), sides[:observations])
    system = system + jnp.where(lane16 == row16, jnp.broadcast_to(errors[:1], row16.shape), 0.0)
    for k in range(observations):
        pivot = system[k : k + 1, :] / system[k : k + 1, k : k + 1]
        system = jnp.where(row16 == k, pivot, system - system[:, k : k + 1] * pivot)
    for m in range(members):
        weights[m, :, :] = jnp.broadcast_to(
            system[:, observations + m : observations + m + 1], (observations, LANES)
        )


def merge_kernel(cap, number, _, *rest):
    parts, gain = rest[:-1], rest[-1]
    size = cap * WINDOW_HEIGHT
    row = (row_index(size) % WINDOW_HEIGHT).astype(jnp.float32)
    column = lane_index(size).astype(jnp.float32)
    row = (row + 0.5 - WINDOW_HEIGHT / 2) / (WINDOW_HEIGHT / 2)
    column = (column + 0.5 - WINDOW_WIDTH / 2) / (WINDOW_WIDTH / 2)
    taper = (1.0 - row * row) * (1.0 - column * column) / (number - 1)
    for k in range(KINDS):
        total = parts[0][k * size : (k + 1) * size, :]
        for more in parts[1:]:
            total = total + more[k * size : (k + 1) * size, :]
        gain[k * size : (k + 1) * size, :] = taper * total
    gain[KINDS * size :, :] = jnp.zeros((8, LANES), jnp.float32)


def apply_kernel(cap, lat, lon, field, mine, theirs, weights, out, work, slots):
    members, _, rows, width = out.shape
    tiles = width // LANES
    size = cap * WINDOW_HEIGHT
    first = lax.axis_index("tile") * rows
    core = lax.axis_index("member") % 2
    count = find_slots(lat, slots, first, rows, cap)
    lane = lane_index()
    patch_row = row_index() < WINDOW_HEIGHT

    def add(layer_of_own):
        def one(s, carry):
            j = slots[s]
            row, block, after, shift = window(lat, lon, j, first, rows, tiles)
            here = patch_row & (lane >= shift)
            there = patch_row & (lane < shift)
            w = [weights[m, pl.ds(j, 1), :] for m in range(members)]
            for l, source in ((layer_of_own, mine), (1 - layer_of_own, theirs)):
                for k in range(KINDS):
                    gain = pltpu.roll(source[pl.ds(k * size + s * 4, 8), :], shift, 1)
                    near = jnp.where(here, gain, 0.0)
                    far = jnp.where(there, gain, 0.0)
                    for m in range(members):
                        f = m * FIELDS + l * KINDS + k
                        work[f, block, pl.ds(row, 8), :] += near * w[m]
                        work[f, after, pl.ds(row, 8), :] += far * w[m]
            return carry

        lax.fori_loop(0, count, one, 0)

    for c in range(2):
        pl.when(core == c)(functools.partial(add, c))
    for f in range(members * FIELDS):
        for i in range(tiles):
            out[f // FIELDS, f % FIELDS, :, i * LANES : (i + 1) * LANES] = work[f, i, PAD : PAD + rows, :]


def partner(size, k):
    if size & (size - 1) == 0:
        return [(i, i ^ k) for i in range(size)]
    return [(i, (i + k) % size) for i in range(size)]


def analyse(cap, shape, field, near, lat, lon, layer, kind, table, value, error, perturb):
    members, _, rows, width = shape
    row_tiles = lax.axis_size("tile")
    devices = lax.axis_size("member")
    chips = devices // 2
    both = 2 * members
    observations = lat.shape[0]
    size = cap * WINDOW_HEIGHT
    part = KINDS * size
    other_core = [(i, i ^ 1) for i in range(devices)]
    slots = pltpu.SMEM((cap + 1,), jnp.int32)
    (obs,) = call(
        functools.partial(observe_kernel, members),
        "observe",
        [SMEM] * 3 + [VMEM] * len(near),
        [(8, LANES)],
    )(layer, kind, table, *near)
    got_obs = lax.ppermute(obs, "member", other_core)
    own, send, sel = call(
        functools.partial(cut_kernel, cap),
        "cut_patches",
        [SMEM] * 2 + [VMEM] * 2,
        [(members * part, LANES), (members * part, LANES), (size, LANES)],
        [slots],
    )(lat, lon, field, obs)
    got = lax.ppermute(send, "member", other_core)
    (seen,) = call(functools.partial(join_kernel, members), "join_observed", [VMEM] * 2, [(8, LANES)])(obs, got_obs)
    seens = [seen] + [lax.ppermute(seen, "member", partner(devices, 2 * k)) for k in range(1, chips)]
    cross, everyone = call(
        functools.partial(moment_kernel, cap, members, chips),
        "moments",
        [VMEM] * (3 + chips),
        [(part, LANES), (chips * both, LANES)],
    )(own, got, sel, *seens)
    crosses = [cross] + [lax.ppermute(cross, "member", partner(devices, 2 * k)) for k in range(1, chips)]
    (weights,) = call(
        weight_kernel,
        "solve_weights",
        [SMEM] * 2 + [VMEM] * 2,
        [(members, observations, LANES)],
    )(value, error, perturb, everyone)
    (mine,) = call(
        functools.partial(merge_kernel, cap, chips * both),
        "merge_moments",
        [VMEM] * (1 + chips),
        [(part + 8, LANES)],
    )(weights, *crosses)
    theirs = lax.ppermute(mine, "member", other_core)
    analysed, _ = call(
        functools.partial(apply_kernel, cap),
        "apply_increments",
        [SMEM] * 2 + [VMEM] * 4,
        [shape, field.shape],
        [slots],
        aliases={2: 1},
    )(lat, lon, field, mine, theirs, weights)
    return analysed


def body(state, vel, band, table, lat, lon, layer, kind, value, error, perturb):
    members, _, rows, width = state.shape
    tiles = width // LANES
    row_tiles = lax.axis_size("tile")
    fields, parts = members * FIELDS, members * 2 * NLAYER
    padded_rows = rows + 2 * PAD
    message = (NEAR_ROWS + tiles * (parts + 2 * fields), LANES)
    out_a, out_b, near = call(
        pack_kernel,
        "pack_edges",
        [HBM] * 6,
        [message, message, (NEAR_ROWS, LANES)],
        [
            pltpu.VMEM((fields, tiles, padded_rows, LANES), jnp.float32),
            pltpu.VMEM((parts, tiles, padded_rows, LANES), jnp.float32),
            pltpu.VMEM((tiles, padded_rows, LANES), jnp.int32),
            pltpu.SMEM(lat.shape, jnp.int32),
            pltpu.SMEM(lon.shape, jnp.int32),
            pltpu.SMEM(kind.shape, jnp.int32),
            pltpu.SemaphoreType.DMA((4 * members * tiles + tiles + 3,)),
        ],
    )(*held(lat, lon, kind, state, vel, band))
    pairs_a = [(i, i + 1) for i in range(0, row_tiles - 1, 2)]
    pairs_b = [(i, i + 1) for i in range(1, row_tiles - 1, 2)]
    from_a = lax.ppermute(out_a, "tile", pairs_a + [(j, i) for i, j in pairs_a])
    from_b = lax.ppermute(out_b, "tile", pairs_b + [(j, i) for i, j in pairs_b])
    wide = pltpu.VMEM((fields, tiles + 2, padded_rows, LANES), jnp.float32)
    inner, own_edge, once_edge, vel_edge, bin_edge = call(
        interior_kernel,
        "interior_rows",
        [HBM] * 4,
        [
            (fields, tiles, padded_rows, LANES),
            (fields, tiles, 8, LANES),
            (fields, tiles, 8, LANES),
            (2, parts, tiles, 8, LANES),
            (tiles, 8, LANES),
        ],
        [
            wide,
            wide,
            pltpu.VMEM((parts, tiles, padded_rows, LANES), jnp.float32),
            pltpu.VMEM(band.shape, jnp.int32),
            pltpu.SMEM(table.shape, jnp.float32),
            pltpu.SemaphoreType.DMA((2 * members * tiles + 2,)),
        ],
        flops=20000000,
    )(*held(table, state, vel, band))
    if row_tiles & (row_tiles - 1) == 0:
        (near,) = call(combine_kernel, "combine_near", [VMEM] * 3, [(NEAR_ROWS, LANES)])(near, from_a, bin_edge)
        step = 2
        while step < row_tiles // 2:
            near = near + lax.ppermute(near, "tile", partner(row_tiles, step))
            step *= 2
        nears = [near] + ([lax.ppermute(near, "tile", partner(row_tiles, step))] if step < row_tiles else [])
    else:
        nears = [lax.psum(near, "tile")]
    narrow = pltpu.VMEM((fields, tiles + 2, 8, LANES), jnp.float32)
    halo = pltpu.VMEM((message[0] + 8, LANES), jnp.float32)
    (field,) = call(
        edge_kernel,
        "edge_rows",
        [SMEM] + [VMEM] * 8,
        [(fields, tiles, padded_rows, LANES)],
        [narrow, narrow, halo, halo],
        aliases={7: 0},
    )(table, own_edge, once_edge, vel_edge, bin_edge, from_a, from_b, inner, near)
    return analyse(CAP, state.shape, field, nears, lat, lon, layer, kind, table, value, error, perturb)


def solution(mesh):
    placed = (
        P("member", None, "tile", None),
        P("member", None, "tile", None),
        P("tile", None),
        P(),
        P(),
        P(),
        P(),
        P(),
        P(),
        P(),
        P("member", None),
    )
    return jax.shard_map(
        body, mesh=mesh, in_specs=placed, out_specs=P("member", None, "tile", None), check_vma=False
    )
```

```python
import functools

import jax
import jax.numpy as jnp
from jax import lax
from jax.experimental import pallas as pl
from jax.experimental.pallas import tpu as pltpu
from jax.sharding import PartitionSpec as P

NLAYER = 2
NCLASS = 4
KINDS = NCLASS + 1
FIELDS = NLAYER * KINDS
WINDOW_HEIGHT = 4
WINDOW_WIDTH = 128
DIFFUSION = 0.08
DEPOSIT = 0.5
CAP = 8

LANES = 128
PAD = 8
GROUP = 8
NEAR_ROWS = 48
EXACT = lax.Precision.HIGHEST
MIB = 1024 * 1024

SMEM = pl.BlockSpec(memory_space=pltpu.SMEM)
VMEM = pl.BlockSpec(memory_space=pltpu.VMEM)
HBM = pl.BlockSpec(memory_space=pltpu.HBM)


def call(kernel, name, in_specs, outs, scratch=(), flops=1000, aliases=None, limit=40):
    return pl.pallas_call(
        kernel,
        name=name,
        in_specs=in_specs,
        out_specs=[SMEM if shape == (1,) else VMEM for shape in outs],
        out_shape=[jax.ShapeDtypeStruct(shape, jnp.int32 if shape == (1,) else jnp.float32) for shape in outs],
        scratch_shapes=list(scratch),
        input_output_aliases=aliases or {},
        compiler_params=pltpu.CompilerParams(vmem_limit_bytes=limit * MIB),
        cost_estimate=pl.CostEstimate(flops=flops, bytes_accessed=1000, transcendentals=0),
    )


def held(*arrays):
    return [pltpu.with_memory_space_constraint(array, pltpu.HBM) for array in arrays]


def lane_index(rows=8):
    return lax.broadcasted_iota(jnp.int32, (rows, LANES), 1)


def row_index(rows=8):
    return lax.broadcasted_iota(jnp.int32, (rows, LANES), 0)


def spread(ref, group, rows=8):
    index = lane_index(rows) // group
    total = jnp.zeros((rows, LANES), ref.dtype)
    for j in range(ref.shape[0]):
        total = jnp.where(index == j, ref[j], total)
    return total


def find_slots(lat, slots, first, rows, cap):
    for s in range(cap + 1):
        slots[s] = 0
    count = jnp.int32(0)
    for j in range(lat.shape[0]):
        start = lat[j] - WINDOW_HEIGHT // 2 - first
        slots[jnp.minimum(count, cap)] = j
        count = count + ((start < rows) & (start + WINDOW_HEIGHT > 0)).astype(jnp.int32)
    return jnp.minimum(count, cap)


def window(lat, lon, j, first, rows, tiles):
    row = jnp.clip(lat[j] - WINDOW_HEIGHT // 2 - first, -WINDOW_HEIGHT, rows) + PAD
    left = lon[j] - WINDOW_WIDTH // 2
    block = left // LANES
    return row, block, jnp.minimum(block + 1, tiles - 1), left % LANES


def coefficients(u, w):
    return (
        (1.0 - 4.0 * DIFFUSION) - (jnp.abs(u) + jnp.abs(w)),
        jnp.maximum(u, 0.0) + DIFFUSION,
        DIFFUSION - jnp.minimum(u, 0.0),
        jnp.maximum(w, 0.0) + DIFFUSION,
        DIFFUSION - jnp.minimum(w, 0.0),
    )


def stencil(coef, centre, up, down, left, right):
    return (coef[0] * centre + coef[1] * up) + (coef[2] * down + coef[3] * left) + coef[4] * right


def choose(values, pick):
    total = jnp.zeros((values.shape[0], LANES), jnp.float32)
    for _ in range(3):
        part = values.astype(jnp.bfloat16)
        total = total + jnp.dot(part, pick, preferred_element_type=jnp.float32)
        values = values - part.astype(jnp.float32)
    return total


def lane_tiles(source, target, members, tiles, each, rows, shift):
    return [
        (
            source.at[m, :, :, pl.ds(i * LANES, LANES)],
            target.at[pl.ds(m * each, each), i + shift, pl.ds(PAD, rows), :],
        )
        for m in range(members)
        for i in range(tiles)
    ]


def start_copies(moves, sems):
    copies = [pltpu.make_async_copy(src, dst, sems.at[n]) for n, (src, dst) in enumerate(moves)]
    for copy in copies:
        copy.start()
    return copies


def pack_kernel(lat_hbm, lon_hbm, kind_hbm, state_hbm, vel_hbm, band_hbm, out_a, out_b, near, s0, vs, bs, lat, lon, kind, sems):
    members, _, rows, width = state_hbm.shape
    tiles = width // LANES
    fields, parts = members * FIELDS, members * 2 * NLAYER
    moves = lane_tiles(state_hbm, s0, members, tiles, FIELDS, rows, 0)
    moves += lane_tiles(vel_hbm, vs, members, tiles, 2 * NLAYER, rows, 0)
    moves += [(band_hbm.at[:, pl.ds(i * LANES, LANES)], bs.at[i, pl.ds(PAD, rows), :]) for i in range(tiles)]
    moves += [(lat_hbm, lat), (lon_hbm, lon), (kind_hbm, kind)]
    copies = start_copies(moves, sems)
    tile = lax.axis_index("tile")
    even = tile % 2 == 0
    first = tile * rows
    zero = jnp.zeros((PAD, LANES), jnp.float32)
    for ref in (s0, vs, bs):
        for n in range(ref.shape[0]) if ref is not bs else (None,):
            for i in range(tiles):
                lead = (i,) if n is None else (n, i)
                ref[lead + (slice(0, PAD),)] = zero.astype(ref.dtype)
                ref[lead + (slice(PAD + rows, None),)] = zero.astype(ref.dtype)
    for copy in copies:
        copy.wait()

    def edge(out, q_first, v_at):
        for i in range(tiles):
            for c in range(parts):
                to = NEAR_ROWS + i * parts + c
                out[to : to + 1, :] = vs[c, i, v_at : v_at + 1, :]
            for f in range(fields):
                to = NEAR_ROWS + tiles * parts + (i * fields + f) * 2
                out[to : to + 2, :] = s0[f, i, q_first : q_first + 2, :]

    top, bottom = PAD, PAD + rows

    @pl.when(even)
    def _():
        edge(out_a, bottom - 2, bottom - 1)
        edge(out_b, top, top)

    @pl.when(jnp.logical_not(even))
    def _():
        edge(out_a, top, top)
        edge(out_b, bottom - 2, bottom - 1)

    lane = lane_index()
    row = row_index()
    blank = jnp.zeros((8, LANES), jnp.float32)
    pairs = members * NLAYER
    qs, us, ws, bins = [blank] * pairs, [blank] * pairs, [blank] * pairs, blank
    for j in range(lat.shape[0]):
        start = jnp.clip(lat[j] - 2 - first, -PAD, rows) + PAD
        left = lon[j] - 2
        block, shift = left // LANES, left % LANES
        after = jnp.minimum(block + 1, tiles - 1)
        turn = (GROUP * j - shift + LANES) % LANES
        here = lane >= shift
        mine = (lane // GROUP) == j

        def fetch(ref, old, *lead):
            both = jnp.where(
                here, ref[lead + (block, pl.ds(start, 8))], ref[lead + (after, pl.ds(start, 8))]
            )
            return jnp.where(mine, pltpu.roll(both.astype(jnp.float32), turn, 1), old)

        for m in range(members):
            for l in range(NLAYER):
                s = m * NLAYER + l
                qs[s] = fetch(s0, qs[s], m * FIELDS + l * KINDS + kind[j])
                us[s] = fetch(vs, us[s], 2 * s)
                ws[s] = fetch(vs, ws[s], 2 * s + 1)
        bins = fetch(bs, bins)

    blocks = [jnp.where(row < 5, q, pltpu.roll(u, 4, 0)) for q, u in zip(qs, us)]
    for m in range(members):
        w = jnp.where(row < 4, ws[2 * m], pltpu.roll(ws[2 * m + 1], 4, 0))
        blocks.append(jnp.where(row == 0, pltpu.roll(bins, 6, 0), w))
    for n, block in enumerate(blocks):
        for out in (near, out_a, out_b):
            out[8 * n : 8 * n + 8, :] = block


def combine_kernel(near, from_a, _, out):
    out[...] = near[...] + from_a[:NEAR_ROWS, :]


def advance(source, f, i, r, coef, lane):
    centre = source[f, i + 1, r : r + 8, :]
    up = source[f, i + 1, r - 1 : r + 7, :]
    down = source[f, i + 1, r + 1 : r + 9, :]
    left, right = sides_of(source[f, i, r : r + 8, :], centre, source[f, i + 2, r : r + 8, :], lane)
    return stencil(coef, centre, up, down, left, right)


def sides_of(before, centre, after, lane):
    left = pltpu.roll(jnp.where(lane == LANES - 1, before, centre), 1, 1)
    right = pltpu.roll(jnp.where(lane == 0, after, centre), LANES - 1, 1)
    return left, right


def settle(a, b, bins, table, k):
    if k == 0:
        return a, b
    rate = jnp.full(a.shape, table[0, k - 1], jnp.float32)
    for level in range(1, table.shape[0]):
        rate = jnp.where(bins == level, table[level, k - 1], rate)
    settled = rate * a
    return a - settled, b + settled - DEPOSIT * rate * b


def interior_kernel(row_tiles, lat_hbm, table_hbm, state, vel, band_hbm, padded, own_edge, once_edge, vel_edge, bin_edge, fullest, s0, s1, vs, band, lat, table, sems):
    members, _, rows, width = state.shape
    tiles = width // LANES
    fields, parts = members * FIELDS, members * 2 * NLAYER
    moves = lane_tiles(vel, vs, members, tiles, 2 * NLAYER, rows, 0)
    moves += lane_tiles(state, s0, members, tiles, FIELDS, rows, 1)
    moves += [(band_hbm, band), (lat_hbm, lat), (table_hbm, table)]
    copies = start_copies(moves, sems)
    zero = jnp.zeros((rows + 2 * PAD, LANES), jnp.float32)
    lane = lane_index()
    for f in range(fields):
        for buffer in (s0, s1):
            buffer[f, 0, :, :] = zero
            buffer[f, tiles + 1, :, :] = zero
    for copy in copies:
        copy.wait()

    most = jnp.int32(0)
    for n in range(row_tiles):
        count = jnp.int32(0)
        for j in range(lat.shape[0]):
            start = lat[j] - WINDOW_HEIGHT // 2 - n * rows
            count = count + ((start < rows) & (start + WINDOW_HEIGHT > 0)).astype(jnp.int32)
        most = jnp.maximum(most, count)
    fullest[0] = most

    def first_step(t, carry):
        ml, i = t // tiles, t % tiles
        for r in range(PAD, PAD + rows, 8):
            coef = coefficients(vs[2 * ml, i, r : r + 8, :], vs[2 * ml + 1, i, r : r + 8, :])
            for k in range(KINDS):
                s1[ml * KINDS + k, i + 1, r : r + 8, :] = advance(s0, ml * KINDS + k, i, r, coef, lane)
        return carry

    for t in range(members * NLAYER * tiles):
        first_step(t, 0)

    def second_step(t, carry):
        m, i = t // tiles, t % tiles
        lanes = pl.ds(i * LANES, LANES)
        for r in range(PAD, PAD + rows, 8):
            coefs = []
            for l in range(NLAYER):
                mc = (m * NLAYER + l) * 2
                coefs.append(coefficients(vs[mc, i, r : r + 8, :], vs[mc + 1, i, r : r + 8, :]))
            bins = band[r - PAD : r - PAD + 8, lanes]
            for k in range(KINDS):
                upper = m * FIELDS + k
                lower = upper + KINDS
                a = advance(s1, upper, i, r, coefs[0], lane)
                b = advance(s1, lower, i, r, coefs[1], lane)
                a, b = settle(a, b, bins, table, k)
                padded[upper, i, r : r + 8, :] = a
                padded[lower, i, r : r + 8, :] = b
        return carry

    for t in range(members * tiles):
        second_step(t, 0)

    top, bottom = PAD, PAD + rows
    half = row_index() < 4

    def halves(ref, lead, low, high):
        return jnp.where(half, ref[lead + (slice(low, low + 8), slice(None))], ref[lead + (slice(high - 4, high + 4), slice(None))])

    for i in range(tiles):
        for f in range(fields):
            padded[f, i, :PAD, :] = zero[:PAD]
            padded[f, i, PAD + rows :, :] = zero[:PAD]
            own_edge[f, i, :, :] = halves(s0, (f, i + 1), top - 2, bottom - 2)
            once_edge[f, i, :, :] = halves(s1, (f, i + 1), top - 1, bottom - 3)
        for c in range(parts):
            vel_edge[0, c, i, :, :] = halves(vs, (c, i), top - 2, bottom - 2)
            vel_edge[1, c, i, :, :] = halves(vs, (c, i), top - 1, bottom - 3)
        upper = band[0:8, i * LANES : (i + 1) * LANES].astype(jnp.float32)
        lower = band[rows - 8 : rows, i * LANES : (i + 1) * LANES].astype(jnp.float32)
        bin_edge[i, :, :] = jnp.where(half, pltpu.roll(upper, 1, 0), pltpu.roll(lower, 7, 0))


def observe_kernel(members, layer, kind, table, *rest):
    parts, out = rest[:-1], rest[-1]
    pairs = members * NLAYER
    blocks = []
    for n in range(pairs + members):
        block = parts[0][8 * n : 8 * n + 8, :]
        for more in parts[1:]:
            block = block + more[8 * n : 8 * n + 8, :]
        blocks.append(block)
    bins = jnp.broadcast_to(blocks[pairs][:1], (8, LANES))
    kinds = spread(kind, GROUP)
    layers = spread(layer, GROUP)
    rate = jnp.zeros((8, LANES), jnp.float32)
    for level in range(table.shape[0]):
        here = jnp.abs(bins - level) < 0.5
        for k in range(NCLASS):
            rate = jnp.where(here & (kinds == k + 1), table[level, k], rate)
    row = row_index()

    def step(q, coef):
        return stencil(
            coef,
            q,
            pltpu.roll(q, 1, 0),
            pltpu.roll(q, 7, 0),
            pltpu.roll(q, 1, 1),
            pltpu.roll(q, LANES - 1, 1),
        )

    seen = jnp.zeros((8, LANES), jnp.float32)
    for m in range(members):
        values = []
        for l in range(NLAYER):
            q = blocks[m * NLAYER + l]
            u = pltpu.roll(q, 4, 0)
            w = blocks[pairs + m]
            coef = coefficients(u, w if l == 0 else pltpu.roll(w, 4, 0))
            values.append(step(step(q, coef), coef))
        a, b = values
        settled = rate * a
        value = jnp.where(layers == 0, a - settled, b + settled - DEPOSIT * rate * b)
        seen = jnp.where(row == m, pltpu.roll(value, (m - 2) % 8, 0), seen)
    squeeze = (
        lax.broadcasted_iota(jnp.int32, (LANES, LANES), 0)
        == lax.broadcasted_iota(jnp.int32, (LANES, LANES), 1) * GROUP + 2
    ).astype(jnp.bfloat16)
    out[...] = choose(seen, squeeze)


def join_kernel(members, obs, got, out):
    out[...] = jnp.where(row_index() < members, obs[...], pltpu.roll(got[...], members, 0))


def edge_kernel(table, own_edge, once_edge, vel_edge, bin_edge, from_a, from_b, inner, near, padded, e0, e1, up, down):
    fields, tiles, padded_rows, _ = padded.shape
    rows = padded_rows - 2 * PAD
    members = fields // FIELDS
    parts = members * 2 * NLAYER
    tile = lax.axis_index("tile")
    count_tiles = lax.axis_size("tile")
    even = tile % 2 == 0
    sent = from_a.shape[0]

    @pl.when(even)
    def _():
        down[:sent, :] = from_a[...]
        up[:sent, :] = from_b[...]

    @pl.when(jnp.logical_not(even))
    def _():
        up[:sent, :] = from_a[...]
        down[:sent, :] = from_b[...]

    lane = lane_index()
    row = row_index()
    zero = jnp.zeros((8, LANES), jnp.float32)
    v_base = NEAR_ROWS
    q_base = NEAR_ROWS + tiles * parts
    for f in range(fields):
        for buffer in (e0, e1):
            buffer[f, 0, :, :] = zero
            buffer[f, tiles + 1, :, :] = zero

    def gather(i, carry):
        for f in range(fields):
            at = q_base + (i * fields + f) * 2
            q = jnp.where(row < 2, up[pl.ds(at, 8), :], own_edge[f, i, :, :])
            e0[f, i + 1, :, :] = jnp.where(row > 5, down[pl.ds(at - 6, 8), :], q)
        return carry

    for i in range(tiles):
        gather(i, 0)
    outside = ((row == 0) & (tile == 0)) | ((row == 7) & (tile == count_tiles - 1))

    def first_step(t, carry):
        ml, i = t // tiles, t % tiles
        flow = []
        for c in range(2):
            at = v_base + i * parts + 2 * ml + c
            v = jnp.where(row == 1, up[pl.ds(at - 1, 8), :], vel_edge[0, 2 * ml + c, i, :, :])
            flow.append(jnp.where(row == 6, down[pl.ds(at - 6, 8), :], v))
        coef = coefficients(*flow)
        for k in range(KINDS):
            f = ml * KINDS + k
            centre = e0[f, i + 1, :, :]
            left, right = sides_of(e0[f, i, :, :], centre, e0[f, i + 2, :, :], lane)
            q = stencil(coef, centre, pltpu.roll(centre, 1, 0), pltpu.roll(centre, 7, 0), left, right)
            q = jnp.where(row < 2, pltpu.roll(q, 7, 0), jnp.where(row > 5, pltpu.roll(q, 1, 0), once_edge[f, i, :, :]))
            e1[f, i + 1, :, :] = jnp.where(outside, 0.0, q)
        return carry

    for t in range(members * NLAYER * tiles):
        first_step(t, 0)

    def second_step(t, carry):
        m, i = t // tiles, t % tiles
        bins = bin_edge[i, :, :].astype(jnp.int32)
        values = []
        for l in range(NLAYER):
            mc = (m * NLAYER + l) * 2
            coef = coefficients(vel_edge[1, mc, i, :, :], vel_edge[1, mc + 1, i, :, :])
            for k in range(KINDS):
                f = m * FIELDS + l * KINDS + k
                centre = e1[f, i + 1, :, :]
                left, right = sides_of(e1[f, i, :, :], centre, e1[f, i + 2, :, :], lane)
                values.append(
                    stencil(coef, centre, pltpu.roll(centre, 1, 0), pltpu.roll(centre, 7, 0), left, right)
                )
        for k in range(KINDS):
            for l, q in enumerate(settle(values[k], values[KINDS + k], bins, table, k)):
                f = m * FIELDS + l * KINDS + k
                padded[f, i, PAD : PAD + 2, :] = q[1:3]
                padded[f, i, PAD + rows - 2 : PAD + rows, :] = q[5:7]
        return carry

    for t in range(members * tiles):
        second_step(t, 0)


def cut_kernel(cap, lat, lon, padded, _, own, send, sel, slots):
    fields, tiles, padded_rows, _ = padded.shape
    rows = padded_rows - 2 * PAD
    members = fields // FIELDS
    core = lax.axis_index("member") % 2
    first = lax.axis_index("tile") * rows
    lane = lane_index()
    size = cap * WINDOW_HEIGHT
    count = find_slots(lat, slots, first, rows, cap)
    for s in range(cap):
        sel[s * 4 : s * 4 + 4, :] = (lane[:4] == slots[s]).astype(jnp.float32)

    def cut(layer_of_own):
        def one(s, carry):
            row, block, after, shift = window(lat, lon, slots[s], first, rows, tiles)
            here = lane >= shift
            for l, target in ((layer_of_own, own), (1 - layer_of_own, send)):
                for m in range(members):
                    for k in range(KINDS):
                        f = m * FIELDS + l * KINDS + k
                        both = jnp.where(
                            here, padded[f, block, pl.ds(row, 8), :], padded[f, after, pl.ds(row, 8), :]
                        )
                        patch = pltpu.roll(both, (LANES - shift) % LANES, 1)
                        target[pl.ds((m * KINDS + k) * size + s * 4, 4), :] = patch[:4]
            return carry

        lax.fori_loop(0, count, one, 0)

    for c in range(2):
        pl.when(core == c)(functools.partial(cut, c))


def moment_kernel(cap, members, chips, own, got, sel, *rest):
    seens, (cross, everyone) = rest[:chips], rest[chips:]
    size = cap * WINDOW_HEIGHT
    part = KINDS * size
    both = 2 * members
    for c, seen in enumerate(seens):
        everyone[c * both : (c + 1) * both, :] = seen[:both, :]
    mean = jnp.sum(everyone[...], axis=0, keepdims=True) / (chips * both)
    sources = [(own, m, m) for m in range(members)] + [(got, m, members + m) for m in range(members)]
    weight = [
        jnp.sum(sel[...] * (everyone[o : o + 1, :] - mean), axis=1, keepdims=True) for _, _, o in sources
    ]
    for k in range(KINDS):
        total = jnp.zeros((size, LANES), jnp.float32)
        for (ref, m, _), o in zip(sources, weight):
            total = total + ref[m * part + k * size : m * part + (k + 1) * size, :] * o
        cross[k * size : (k + 1) * size, :] = total


def weight_kernel(value, error, perturb, everyone_ref, weights):
    members, observations = perturb.shape
    everyone = everyone_ref[...]
    number = everyone.shape[0]
    anomaly = everyone - jnp.sum(everyone, axis=0, keepdims=True) / number
    over = (((0,), (0,)), ((), ()))
    cov = lax.dot_general(anomaly, anomaly, over, precision=EXACT, preferred_element_type=jnp.float32)
    row16 = row_index(observations)
    lane16 = lane_index(observations)
    errors = spread(error, 1)
    innovation = spread(value, 1)[:members] - everyone[:members]
    noise = jnp.concatenate(
        [perturb[...], jnp.zeros((members, LANES - observations), jnp.float32)], axis=1
    )
    innovation = innovation + jnp.sqrt(errors[:members]) * noise
    place = (lane_index(members) == row_index(members) + observations).astype(jnp.float32)
    sides = lax.dot_general(innovation, place, over, precision=EXACT, preferred_element_type=jnp.float32)
    system = jnp.where(lane16 < observations, cov[:observations] / (number - 1), sides[:observations])
    system = system + jnp.where(lane16 == row16, jnp.broadcast_to(errors[:1], row16.shape), 0.0)
    for k in range(observations):
        pivot = system[k : k + 1, :] / system[k : k + 1, k : k + 1]
        system = jnp.where(row16 == k, pivot, system - system[:, k : k + 1] * pivot)
    for m in range(members):
        weights[m, :, :] = jnp.broadcast_to(
            system[:, observations + m : observations + m + 1], (observations, LANES)
        )


def merge_kernel(cap, number, _, *rest):
    parts, gain = rest[:-1], rest[-1]
    size = cap * WINDOW_HEIGHT
    row = (row_index(size) % WINDOW_HEIGHT).astype(jnp.float32)
    column = lane_index(size).astype(jnp.float32)
    row = (row + 0.5 - WINDOW_HEIGHT / 2) / (WINDOW_HEIGHT / 2)
    column = (column + 0.5 - WINDOW_WIDTH / 2) / (WINDOW_WIDTH / 2)
    taper = (1.0 - row * row) * (1.0 - column * column) / (number - 1)
    for k in range(KINDS):
        total = parts[0][k * size : (k + 1) * size, :]
        for more in parts[1:]:
            total = total + more[k * size : (k + 1) * size, :]
        gain[k * size : (k + 1) * size, :] = taper * total
    gain[KINDS * size :, :] = jnp.zeros((8, LANES), jnp.float32)


def apply_kernel(cap, lat, lon, field, mine, theirs, weights, out, work, slots):
    members, _, rows, width = out.shape
    tiles = width // LANES
    size = cap * WINDOW_HEIGHT
    first = lax.axis_index("tile") * rows
    core = lax.axis_index("member") % 2
    count = find_slots(lat, slots, first, rows, cap)
    lane = lane_index()
    patch_row = row_index() < WINDOW_HEIGHT

    def add(layer_of_own):
        def one(s, carry):
            j = slots[s]
            row, block, after, shift = window(lat, lon, j, first, rows, tiles)
            here = patch_row & (lane >= shift)
            there = patch_row & (lane < shift)
            w = [weights[m, pl.ds(j, 1), :] for m in range(members)]
            for l, source in ((layer_of_own, mine), (1 - layer_of_own, theirs)):
                for k in range(KINDS):
                    gain = pltpu.roll(source[pl.ds(k * size + s * 4, 8), :], shift, 1)
                    near = jnp.where(here, gain, 0.0)
                    far = jnp.where(there, gain, 0.0)
                    for m in range(members):
                        f = m * FIELDS + l * KINDS + k
                        work[f, block, pl.ds(row, 8), :] += near * w[m]
                        work[f, after, pl.ds(row, 8), :] += far * w[m]
            return carry

        lax.fori_loop(0, count, one, 0)

    for c in range(2):
        pl.when(core == c)(functools.partial(add, c))
    for f in range(members * FIELDS):
        for i in range(tiles):
            out[f // FIELDS, f % FIELDS, :, i * LANES : (i + 1) * LANES] = work[f, i, PAD : PAD + rows, :]


def partner(size, k):
    if size & (size - 1) == 0:
        return [(i, i ^ k) for i in range(size)]
    return [(i, (i + k) % size) for i in range(size)]


def analyse(cap, shape, field, near, lat, lon, layer, kind, table, value, error, perturb):
    members, _, rows, width = shape
    row_tiles = lax.axis_size("tile")
    devices = lax.axis_size("member")
    chips = devices // 2
    both = 2 * members
    observations = lat.shape[0]
    size = cap * WINDOW_HEIGHT
    part = KINDS * size
    other_core = [(i, i ^ 1) for i in range(devices)]
    slots = pltpu.SMEM((cap + 1,), jnp.int32)
    (obs,) = call(
        functools.partial(observe_kernel, members),
        "observe",
        [SMEM] * 3 + [VMEM] * len(near),
        [(8, LANES)],
    )(layer, kind, table, *near)
    got_obs = lax.ppermute(obs, "member", other_core)
    own, send, sel = call(
        functools.partial(cut_kernel, cap),
        "cut_patches",
        [SMEM] * 2 + [VMEM] * 2,
        [(members * part, LANES), (members * part, LANES), (size, LANES)],
        [slots],
    )(lat, lon, field, obs)
    got = lax.ppermute(send, "member", other_core)
    (seen,) = call(functools.partial(join_kernel, members), "join_observed", [VMEM] * 2, [(8, LANES)])(obs, got_obs)
    seens = [seen] + [lax.ppermute(seen, "member", partner(devices, 2 * k)) for k in range(1, chips)]
    cross, everyone = call(
        functools.partial(moment_kernel, cap, members, chips),
        "moments",
        [VMEM] * (3 + chips),
        [(part, LANES), (chips * both, LANES)],
    )(own, got, sel, *seens)
    crosses = [cross] + [lax.ppermute(cross, "member", partner(devices, 2 * k)) for k in range(1, chips)]
    (weights,) = call(
        weight_kernel,
        "solve_weights",
        [SMEM] * 2 + [VMEM] * 2,
        [(members, observations, LANES)],
    )(value, error, perturb, everyone)
    (mine,) = call(
        functools.partial(merge_kernel, cap, chips * both),
        "merge_moments",
        [VMEM] * (1 + chips),
        [(part + 8, LANES)],
    )(weights, *crosses)
    theirs = lax.ppermute(mine, "member", other_core)
    analysed, _ = call(
        functools.partial(apply_kernel, cap),
        "apply_increments",
        [SMEM] * 2 + [VMEM] * 4,
        [shape, field.shape],
        [slots],
        aliases={2: 1},
    )(lat, lon, field, mine, theirs, weights)
    return analysed


def body(state, vel, band, table, lat, lon, layer, kind, value, error, perturb):
    members, _, rows, width = state.shape
    tiles = width // LANES
    row_tiles = lax.axis_size("tile")
    fields, parts = members * FIELDS, members * 2 * NLAYER
    padded_rows = rows + 2 * PAD
    message = (NEAR_ROWS + tiles * (parts + 2 * fields), LANES)
    out_a, out_b, near = call(
        pack_kernel,
        "pack_edges",
        [HBM] * 6,
        [message, message, (NEAR_ROWS, LANES)],
        [
            pltpu.VMEM((fields, tiles, padded_rows, LANES), jnp.float32),
            pltpu.VMEM((parts, tiles, padded_rows, LANES), jnp.float32),
            pltpu.VMEM((tiles, padded_rows, LANES), jnp.int32),
            pltpu.SMEM(lat.shape, jnp.int32),
            pltpu.SMEM(lon.shape, jnp.int32),
            pltpu.SMEM(kind.shape, jnp.int32),
            pltpu.SemaphoreType.DMA((4 * members * tiles + tiles + 3,)),
        ],
    )(*held(lat, lon, kind, state, vel, band))
    pairs_a = [(i, i + 1) for i in range(0, row_tiles - 1, 2)]
    pairs_b = [(i, i + 1) for i in range(1, row_tiles - 1, 2)]
    from_a = lax.ppermute(out_a, "tile", pairs_a + [(j, i) for i, j in pairs_a])
    from_b = lax.ppermute(out_b, "tile", pairs_b + [(j, i) for i, j in pairs_b])
    wide = pltpu.VMEM((fields, tiles + 2, padded_rows, LANES), jnp.float32)
    inner, own_edge, once_edge, vel_edge, bin_edge, fullest = call(
        functools.partial(interior_kernel, row_tiles),
        "interior_rows",
        [HBM] * 5,
        [
            (fields, tiles, padded_rows, LANES),
            (fields, tiles, 8, LANES),
            (fields, tiles, 8, LANES),
            (2, parts, tiles, 8, LANES),
            (tiles, 8, LANES),
            (1,),
        ],
        [
            wide,
            wide,
            pltpu.VMEM((parts, tiles, padded_rows, LANES), jnp.float32),
            pltpu.VMEM(band.shape, jnp.int32),
            pltpu.SMEM(lat.shape, jnp.int32),
            pltpu.SMEM(table.shape, jnp.float32),
            pltpu.SemaphoreType.DMA((2 * members * tiles + 3,)),
        ],
        flops=20000000,
    )(*held(lat, table, state, vel, band))
    if row_tiles & (row_tiles - 1) == 0:
        (near,) = call(combine_kernel, "combine_near", [VMEM] * 3, [(NEAR_ROWS, LANES)])(near, from_a, bin_edge)
        step = 2
        while step < row_tiles // 2:
            near = near + lax.ppermute(near, "tile", partner(row_tiles, step))
            step *= 2
        nears = [near] + ([lax.ppermute(near, "tile", partner(row_tiles, step))] if step < row_tiles else [])
    else:
        nears = [lax.psum(near, "tile")]
    narrow = pltpu.VMEM((fields, tiles + 2, 8, LANES), jnp.float32)
    halo = pltpu.VMEM((message[0] + 8, LANES), jnp.float32)
    (field,) = call(
        edge_kernel,
        "edge_rows",
        [SMEM] + [VMEM] * 8,
        [(fields, tiles, padded_rows, LANES)],
        [narrow, narrow, halo, halo],
        aliases={7: 0},
    )(table, own_edge, once_edge, vel_edge, bin_edge, from_a, from_b, inner, near)
    operands = (field, nears, lat, lon, layer, kind, table, value, error, perturb)
    return lax.cond(
        fullest[0] <= CAP,
        functools.partial(analyse, CAP, state.shape),
        functools.partial(analyse, lat.shape[0], state.shape),
        *operands,
    )


def solution(mesh):
    placed = (
        P("member", None, "tile", None),
        P("member", None, "tile", None),
        P("tile", None),
        P(),
        P(),
        P(),
        P(),
        P(),
        P(),
        P(),
        P("member", None),
    )
    return jax.shard_map(
        body, mesh=mesh, in_specs=placed, out_specs=P("member", None, "tile", None), check_vma=False
    )
```

```python
import functools

import jax
import jax.numpy as jnp
from jax import lax
from jax.experimental import pallas as pl
from jax.experimental.pallas import tpu as pltpu
from jax.sharding import PartitionSpec as P

NLAYER = 2
NCLASS = 4
KINDS = NCLASS + 1
FIELDS = NLAYER * KINDS
WINDOW_HEIGHT = 4
WINDOW_WIDTH = 128
DIFFUSION = 0.08
DEPOSIT = 0.5
CAPS = (6, 7, 8, 10)

LANES = 128
PAD = 8
GROUP = 8
NEAR_ROWS = 48
EXACT = lax.Precision.HIGHEST
MIB = 1024 * 1024

SMEM = pl.BlockSpec(memory_space=pltpu.SMEM)
VMEM = pl.BlockSpec(memory_space=pltpu.VMEM)
HBM = pl.BlockSpec(memory_space=pltpu.HBM)


def call(kernel, name, in_specs, outs, scratch=(), flops=1000, aliases=None, limit=40, out_space=VMEM):
    return pl.pallas_call(
        kernel,
        name=name,
        in_specs=in_specs,
        out_specs=[SMEM if shape == (1,) else out_space for shape in outs],
        out_shape=[
            shape
            if isinstance(shape, jax.ShapeDtypeStruct)
            else jax.ShapeDtypeStruct(shape, jnp.int32 if shape == (1,) else jnp.float32)
            for shape in outs
        ],
        scratch_shapes=list(scratch),
        input_output_aliases=aliases or {},
        compiler_params=pltpu.CompilerParams(vmem_limit_bytes=limit * MIB),
        cost_estimate=pl.CostEstimate(flops=flops, bytes_accessed=1000, transcendentals=0),
    )


def held(*arrays):
    return [pltpu.with_memory_space_constraint(array, pltpu.HBM) for array in arrays]


def lane_index(rows=8):
    return lax.broadcasted_iota(jnp.int32, (rows, LANES), 1)


def row_index(rows=8):
    return lax.broadcasted_iota(jnp.int32, (rows, LANES), 0)


def spread(ref, group, rows=8):
    index = lane_index(rows) // group
    total = jnp.zeros((rows, LANES), ref.dtype)
    for j in range(ref.shape[0]):
        total = jnp.where(index == j, ref[j], total)
    return total


def find_slots(lat, slots, first, rows, cap):
    for s in range(cap + 1):
        slots[s] = 0
    count = jnp.int32(0)
    for j in range(lat.shape[0]):
        start = lat[j] - WINDOW_HEIGHT // 2 - first
        slots[jnp.minimum(count, cap)] = j
        count = count + ((start < rows) & (start + WINDOW_HEIGHT > 0)).astype(jnp.int32)
    return jnp.minimum(count, cap)


def window(lat, lon, j, first, rows, tiles):
    row = jnp.clip(lat[j] - WINDOW_HEIGHT // 2 - first, -WINDOW_HEIGHT, rows) + PAD
    left = lon[j] - WINDOW_WIDTH // 2
    block = left // LANES
    return row, block, jnp.minimum(block + 1, tiles - 1), left % LANES


def coefficients(u, w):
    return (
        (1.0 - 4.0 * DIFFUSION) - (jnp.abs(u) + jnp.abs(w)),
        jnp.maximum(u, 0.0) + DIFFUSION,
        DIFFUSION - jnp.minimum(u, 0.0),
        jnp.maximum(w, 0.0) + DIFFUSION,
        DIFFUSION - jnp.minimum(w, 0.0),
    )


def stencil(coef, centre, up, down, left, right):
    return (coef[0] * centre + coef[1] * up) + (coef[2] * down + coef[3] * left) + coef[4] * right


def choose(values, pick):
    total = jnp.zeros((values.shape[0], LANES), jnp.float32)
    for _ in range(3):
        part = values.astype(jnp.bfloat16)
        total = total + jnp.dot(part, pick, preferred_element_type=jnp.float32)
        values = values - part.astype(jnp.float32)
    return total


def lane_tiles(source, target, members, tiles, each, rows, shift):
    return [
        (
            source.at[m, :, :, pl.ds(i * LANES, LANES)],
            target.at[pl.ds(m * each, each), i + shift, pl.ds(PAD, rows), :],
        )
        for m in range(members)
        for i in range(tiles)
    ]


def start_copies(moves, sems):
    copies = [pltpu.make_async_copy(src, dst, sems.at[n]) for n, (src, dst) in enumerate(moves)]
    for copy in copies:
        copy.start()
    return copies


def load_kernel(lat_hbm, lon_hbm, kind_hbm, state_hbm, vel_hbm, band_hbm, out_a, out_b, near, s0, vs, bs, lat, lon, kind, sems):
    members, _, rows, width = state_hbm.shape
    tiles = width // LANES
    fields, parts = members * FIELDS, members * 2 * NLAYER
    moves = lane_tiles(state_hbm, s0, members, tiles, FIELDS, rows, 1)
    moves += lane_tiles(vel_hbm, vs, members, tiles, 2 * NLAYER, rows, 0)
    moves += [(band_hbm.at[:, pl.ds(i * LANES, LANES)], bs.at[i, pl.ds(PAD, rows), :]) for i in range(tiles)]
    moves += [(lat_hbm, lat), (lon_hbm, lon), (kind_hbm, kind)]
    copies = start_copies(moves, sems)
    tile = lax.axis_index("tile")
    first = tile * rows
    even = tile % 2 == 0
    zero = jnp.zeros((PAD, LANES), jnp.float32)
    bands = jnp.zeros((PAD, LANES), jnp.int32)
    for i in range(tiles):
        for part in (slice(0, PAD), slice(PAD + rows, None)):
            for f in range(fields):
                s0[f, i + 1, part, :] = zero
            for c in range(parts):
                vs[c, i, part, :] = zero
            bs[i, part, :] = bands
    for f in range(fields):
        for r in range(0, rows + 2 * PAD, PAD):
            s0[f, 0, r : r + PAD, :] = zero
            s0[f, tiles + 1, r : r + PAD, :] = zero
    for copy in copies:
        copy.wait()

    def edge(out, q_first, v_at):
        for i in range(tiles):
            for c in range(parts):
                to = i * parts + c
                out[to : to + 1, :] = vs[c, i, v_at : v_at + 1, :]
            for f in range(fields):
                to = tiles * parts + (i * fields + f) * 2
                out[to : to + 2, :] = s0[f, i + 1, q_first : q_first + 2, :]

    top, bottom = PAD, PAD + rows

    @pl.when(even)
    def _():
        edge(out_a, bottom - 2, bottom - 1)
        edge(out_b, top, top)

    @pl.when(jnp.logical_not(even))
    def _():
        edge(out_a, top, top)
        edge(out_b, bottom - 2, bottom - 1)

    lane = lane_index()
    row = row_index()
    blank = jnp.zeros((8, LANES), jnp.float32)
    pairs = members * NLAYER
    qs, us, ws, bins = [blank] * pairs, [blank] * pairs, [blank] * pairs, blank
    for j in range(lat.shape[0]):
        start = jnp.clip(lat[j] - 2 - first, -PAD, rows) + PAD
        left = lon[j] - 2
        block, shift = left // LANES, left % LANES
        after = jnp.minimum(block + 1, tiles - 1)
        turn = (GROUP * j - shift + LANES) % LANES
        here = lane >= shift
        mine = (lane // GROUP) == j

        def fetch(ref, old, *lead, by=0):
            both = jnp.where(
                here, ref[lead + (block + by, pl.ds(start, 8))], ref[lead + (after + by, pl.ds(start, 8))]
            )
            return jnp.where(mine, pltpu.roll(both.astype(jnp.float32), turn, 1), old)

        for m in range(members):
            for l in range(NLAYER):
                s = m * NLAYER + l
                qs[s] = fetch(s0, qs[s], m * FIELDS + l * KINDS + kind[j], by=1)
                us[s] = fetch(vs, us[s], 2 * s)
                ws[s] = fetch(vs, ws[s], 2 * s + 1)
        bins = fetch(bs, bins)

    blocks = [jnp.where(row < 5, q, pltpu.roll(u, 4, 0)) for q, u in zip(qs, us)]
    for m in range(members):
        w = jnp.where(row < 4, ws[2 * m], pltpu.roll(ws[2 * m + 1], 4, 0))
        blocks.append(jnp.where(row == 0, pltpu.roll(bins, 6, 0), w))
    for n, block in enumerate(blocks):
        near[8 * n : 8 * n + 8, :] = block
        base = tiles * (parts + 2 * fields) + 8 * n
        out_a[base : base + 8, :] = block


def combine_kernel(near, from_a, _, out):
    out[...] = near[...] + from_a[from_a.shape[0] - NEAR_ROWS :, :]


def advance(source, f, i, r, coef, lane):
    centre = source[f, i + 1, r : r + 8, :]
    up = source[f, i + 1, r - 1 : r + 7, :]
    down = source[f, i + 1, r + 1 : r + 9, :]
    left, right = sides_of(source[f, i, r : r + 8, :], centre, source[f, i + 2, r : r + 8, :], lane)
    return stencil(coef, centre, up, down, left, right)


def sides_of(before, centre, after, lane):
    left = pltpu.roll(jnp.where(lane == LANES - 1, before, centre), 1, 1)
    right = pltpu.roll(jnp.where(lane == 0, after, centre), LANES - 1, 1)
    return left, right


def settle(a, b, bins, table, k):
    if k == 0:
        return a, b
    rate = jnp.full(a.shape, table[0, k - 1], jnp.float32)
    for level in range(1, table.shape[0]):
        rate = jnp.where(bins == level, table[level, k - 1], rate)
    settled = rate * a
    return a - settled, b + settled - DEPOSIT * rate * b


def interior_kernel(row_tiles, rows, caps, lat_hbm, table_hbm, s0, vs, band, padded, own_edge, once_edge, vel_edge, bin_edge, step_of, s1, lat, table, sems):
    fields, tiles, _, _ = padded.shape
    members = fields // FIELDS
    parts = members * 2 * NLAYER
    copies = start_copies([(lat_hbm, lat), (table_hbm, table)], sems)
    zero = jnp.zeros((rows + 2 * PAD, LANES), jnp.float32)
    lane = lane_index()
    for f in range(fields):
        s1[f, 0, :, :] = zero
        s1[f, tiles + 1, :, :] = zero

    def first_step(t, carry):
        ml, i = t // tiles, t % tiles
        for r in range(PAD, PAD + rows, 8):
            coef = coefficients(vs[2 * ml, i, r : r + 8, :], vs[2 * ml + 1, i, r : r + 8, :])
            for k in range(KINDS):
                s1[ml * KINDS + k, i + 1, r : r + 8, :] = advance(s0, ml * KINDS + k, i, r, coef, lane)
        return carry

    for t in range(members * NLAYER * tiles):
        first_step(t, 0)
    for copy in copies:
        copy.wait()

    most = jnp.int32(0)
    for n in range(row_tiles):
        count = jnp.int32(0)
        for j in range(lat.shape[0]):
            start = lat[j] - WINDOW_HEIGHT // 2 - n * rows
            count = count + ((start < rows) & (start + WINDOW_HEIGHT > 0)).astype(jnp.int32)
        most = jnp.maximum(most, count)
    step_of[0] = sum((most > cap).astype(jnp.int32) for cap in caps)

    def second_step(t, carry):
        m, i = t // tiles, t % tiles
        for r in range(PAD, PAD + rows, 8):
            coefs = []
            for l in range(NLAYER):
                mc = (m * NLAYER + l) * 2
                coefs.append(coefficients(vs[mc, i, r : r + 8, :], vs[mc + 1, i, r : r + 8, :]))
            bins = band[i, r : r + 8, :]
            for k in range(KINDS):
                upper = m * FIELDS + k
                lower = upper + KINDS
                a = advance(s1, upper, i, r, coefs[0], lane)
                b = advance(s1, lower, i, r, coefs[1], lane)
                a, b = settle(a, b, bins, table, k)
                padded[upper, i, r : r + 8, :] = a
                padded[lower, i, r : r + 8, :] = b
        return carry

    for t in range(members * tiles):
        second_step(t, 0)

    top, bottom = PAD, PAD + rows
    half = row_index() < 4

    def halves(ref, lead, low, high):
        return jnp.where(half, ref[lead + (slice(low, low + 8), slice(None))], ref[lead + (slice(high - 4, high + 4), slice(None))])

    for i in range(tiles):
        for f in range(fields):
            padded[f, i, :PAD, :] = zero[:PAD]
            padded[f, i, PAD + rows :, :] = zero[:PAD]
            own_edge[f, i, :, :] = halves(s0, (f, i + 1), top - 2, bottom - 2)
            once_edge[f, i, :, :] = halves(s1, (f, i + 1), top - 1, bottom - 3)
        for c in range(parts):
            vel_edge[0, c, i, :, :] = halves(vs, (c, i), top - 2, bottom - 2)
            vel_edge[1, c, i, :, :] = halves(vs, (c, i), top - 1, bottom - 3)
        bin_edge[i, :, :] = halves(band, (i,), top - 1, bottom - 3).astype(jnp.float32)


def observe_kernel(members, layer, kind, table, *rest):
    parts, out = rest[:-1], rest[-1]
    pairs = members * NLAYER
    blocks = []
    for n in range(pairs + members):
        block = parts[0][8 * n : 8 * n + 8, :]
        for more in parts[1:]:
            block = block + more[8 * n : 8 * n + 8, :]
        blocks.append(block)
    bins = jnp.broadcast_to(blocks[pairs][:1], (8, LANES))
    kinds = spread(kind, GROUP)
    layers = spread(layer, GROUP)
    rate = jnp.zeros((8, LANES), jnp.float32)
    for level in range(table.shape[0]):
        here = jnp.abs(bins - level) < 0.5
        for k in range(NCLASS):
            rate = jnp.where(here & (kinds == k + 1), table[level, k], rate)
    row = row_index()

    def step(q, coef):
        return stencil(
            coef,
            q,
            pltpu.roll(q, 1, 0),
            pltpu.roll(q, 7, 0),
            pltpu.roll(q, 1, 1),
            pltpu.roll(q, LANES - 1, 1),
        )

    seen = jnp.zeros((8, LANES), jnp.float32)
    for m in range(members):
        values = []
        for l in range(NLAYER):
            q = blocks[m * NLAYER + l]
            u = pltpu.roll(q, 4, 0)
            w = blocks[pairs + m]
            coef = coefficients(u, w if l == 0 else pltpu.roll(w, 4, 0))
            values.append(step(step(q, coef), coef))
        a, b = values
        settled = rate * a
        value = jnp.where(layers == 0, a - settled, b + settled - DEPOSIT * rate * b)
        seen = jnp.where(row == m, pltpu.roll(value, (m - 2) % 8, 0), seen)
    squeeze = (
        lax.broadcasted_iota(jnp.int32, (LANES, LANES), 0)
        == lax.broadcasted_iota(jnp.int32, (LANES, LANES), 1) * GROUP + 2
    ).astype(jnp.bfloat16)
    out[...] = choose(seen, squeeze)


def edge_kernel(table, own_edge, once_edge, vel_edge, bin_edge, from_a, from_b, inner, near, padded, e0, e1, up, down):
    fields, tiles, padded_rows, _ = padded.shape
    rows = padded_rows - 2 * PAD
    members = fields // FIELDS
    parts = members * 2 * NLAYER
    tile = lax.axis_index("tile")
    count_tiles = lax.axis_size("tile")
    even = tile % 2 == 0
    sent = from_b.shape[0]

    @pl.when(even)
    def _():
        down[PAD : PAD + sent, :] = from_a[:sent, :]
        up[PAD : PAD + sent, :] = from_b[...]

    @pl.when(jnp.logical_not(even))
    def _():
        up[PAD : PAD + sent, :] = from_a[:sent, :]
        down[PAD : PAD + sent, :] = from_b[...]

    for edge_tile, ref in ((0, up), (count_tiles - 1, down)):

        @pl.when(tile == edge_tile)
        def _():
            ref[...] = jnp.zeros(ref.shape, jnp.float32)

    lane = lane_index()
    row = row_index()
    zero = jnp.zeros((8, LANES), jnp.float32)
    v_base = PAD
    q_base = PAD + tiles * parts
    for f in range(fields):
        for buffer in (e0, e1):
            buffer[f, 0, :, :] = zero
            buffer[f, tiles + 1, :, :] = zero

    def gather(i, carry):
        for f in range(fields):
            at = q_base + (i * fields + f) * 2
            q = jnp.where(row < 2, up[pl.ds(at, 8), :], own_edge[f, i, :, :])
            e0[f, i + 1, :, :] = jnp.where(row > 5, down[pl.ds(at - 6, 8), :], q)
        return carry

    for i in range(tiles):
        gather(i, 0)
    outside = ((row == 0) & (tile == 0)) | ((row == 7) & (tile == count_tiles - 1))

    def first_step(t, carry):
        ml, i = t // tiles, t % tiles
        flow = []
        for c in range(2):
            at = v_base + i * parts + 2 * ml + c
            v = jnp.where(row == 1, up[pl.ds(at - 1, 8), :], vel_edge[0, 2 * ml + c, i, :, :])
            flow.append(jnp.where(row == 6, down[pl.ds(at - 6, 8), :], v))
        coef = coefficients(*flow)
        for k in range(KINDS):
            f = ml * KINDS + k
            centre = e0[f, i + 1, :, :]
            left, right = sides_of(e0[f, i, :, :], centre, e0[f, i + 2, :, :], lane)
            q = stencil(coef, centre, pltpu.roll(centre, 1, 0), pltpu.roll(centre, 7, 0), left, right)
            q = jnp.where(row < 2, pltpu.roll(q, 7, 0), jnp.where(row > 5, pltpu.roll(q, 1, 0), once_edge[f, i, :, :]))
            e1[f, i + 1, :, :] = jnp.where(outside, 0.0, q)
        return carry

    for t in range(members * NLAYER * tiles):
        first_step(t, 0)

    def second_step(t, carry):
        m, i = t // tiles, t % tiles
        bins = bin_edge[i, :, :].astype(jnp.int32)
        values = []
        for l in range(NLAYER):
            mc = (m * NLAYER + l) * 2
            coef = coefficients(vel_edge[1, mc, i, :, :], vel_edge[1, mc + 1, i, :, :])
            for k in range(KINDS):
                f = m * FIELDS + l * KINDS + k
                centre = e1[f, i + 1, :, :]
                left, right = sides_of(e1[f, i, :, :], centre, e1[f, i + 2, :, :], lane)
                values.append(
                    stencil(coef, centre, pltpu.roll(centre, 1, 0), pltpu.roll(centre, 7, 0), left, right)
                )
        for k in range(KINDS):
            for l, q in enumerate(settle(values[k], values[KINDS + k], bins, table, k)):
                f = m * FIELDS + l * KINDS + k
                padded[f, i, PAD : PAD + 2, :] = q[1:3]
                padded[f, i, PAD + rows - 2 : PAD + rows, :] = q[5:7]
        return carry

    for t in range(members * tiles):
        second_step(t, 0)


def cut_kernel(cap, lat, lon, padded, obs, own, send, sel, slots):
    fields, tiles, padded_rows, _ = padded.shape
    rows = padded_rows - 2 * PAD
    members = fields // FIELDS
    core = lax.axis_index("member") % 2
    first = lax.axis_index("tile") * rows
    lane = lane_index()
    size = cap * WINDOW_HEIGHT
    count = find_slots(lat, slots, first, rows, cap)
    for s in range(cap):
        sel[s * 4 : s * 4 + 4, :] = (lane[:4] == slots[s]).astype(jnp.float32)
    send[members * KINDS * size :, :] = obs[...]

    def cut(layer_of_own):
        def one(s, carry):
            row, block, after, shift = window(lat, lon, slots[s], first, rows, tiles)
            here = lane >= shift
            for l, target in ((layer_of_own, own), (1 - layer_of_own, send)):
                for m in range(members):
                    for k in range(KINDS):
                        f = m * FIELDS + l * KINDS + k
                        both = jnp.where(
                            here, padded[f, block, pl.ds(row, 8), :], padded[f, after, pl.ds(row, 8), :]
                        )
                        patch = pltpu.roll(both, (LANES - shift) % LANES, 1)
                        target[pl.ds((m * KINDS + k) * size + s * 4, 4), :] = patch[:4]
            return carry

        lax.fori_loop(0, count, one, 0)

    for c in range(2):
        pl.when(core == c)(functools.partial(cut, c))


def pair_kernel(cap, members, own, got, obs, sel, msg):
    size = cap * WINDOW_HEIGHT
    part = KINDS * size
    seen, theirs = obs[:members, :], got[members * part : members * part + members, :]
    mean = (jnp.sum(seen, axis=0, keepdims=True) + jnp.sum(theirs, axis=0, keepdims=True)) / (2 * members)
    sources = [(own, m, seen[m : m + 1]) for m in range(members)]
    sources += [(got, m, theirs[m : m + 1]) for m in range(members)]
    weight = [jnp.sum(sel[...] * (o - mean), axis=1, keepdims=True) for _, _, o in sources]
    for k in range(KINDS):
        cross = jnp.zeros((size, LANES), jnp.float32)
        total = jnp.zeros((size, LANES), jnp.float32)
        for (ref, m, _), o in zip(sources, weight):
            patch = ref[m * part + k * size : m * part + (k + 1) * size, :]
            cross = cross + patch * o
            total = total + patch
        msg[k * size : (k + 1) * size, :] = cross
        msg[part + k * size : part + (k + 1) * size, :] = total
    msg[2 * part :, :] = jnp.zeros((8, LANES), jnp.float32)
    msg[2 * part : 2 * part + members, :] = seen
    msg[2 * part + members : 2 * part + 2 * members, :] = theirs


def weight_kernel(value, error, perturb, everyone_ref, weights):
    members, observations = perturb.shape
    everyone = everyone_ref[...]
    number = everyone.shape[0]
    anomaly = everyone - jnp.sum(everyone, axis=0, keepdims=True) / number
    over = (((0,), (0,)), ((), ()))
    cov = lax.dot_general(anomaly, anomaly, over, precision=EXACT, preferred_element_type=jnp.float32)
    row16 = row_index(observations)
    lane16 = lane_index(observations)
    errors = spread(error, 1)
    innovation = spread(value, 1)[:members] - everyone[:members]
    noise = jnp.concatenate(
        [perturb[...], jnp.zeros((members, LANES - observations), jnp.float32)], axis=1
    )
    innovation = innovation + jnp.sqrt(errors[:members]) * noise
    place = (lane_index(members) == row_index(members) + observations).astype(jnp.float32)
    sides = lax.dot_general(innovation, place, over, precision=EXACT, preferred_element_type=jnp.float32)
    system = jnp.where(lane16 < observations, cov[:observations] / (number - 1), sides[:observations])
    system = system + jnp.where(lane16 == row16, jnp.broadcast_to(errors[:1], row16.shape), 0.0)
    for k in range(observations):
        pivot = system[k : k + 1, :] / system[k : k + 1, k : k + 1]
        system = jnp.where(row16 == k, pivot, system - system[:, k : k + 1] * pivot)
    for m in range(members):
        weights[m, :, :] = jnp.broadcast_to(
            system[:, observations + m : observations + m + 1], (observations, LANES)
        )


def merge_kernel(cap, members, chips, sel, *rest):
    msgs, (gain, everyone) = rest[:chips], rest[chips:]
    size = cap * WINDOW_HEIGHT
    part = KINDS * size
    both = 2 * members
    number = chips * both
    means = []
    for c, msg in enumerate(msgs):
        seen = msg[2 * part : 2 * part + both, :]
        everyone[c * both : (c + 1) * both, :] = seen
        means.append(jnp.sum(seen, axis=0, keepdims=True) / both)
    mean = functools.reduce(jnp.add, means) / chips
    shifts = [jnp.sum(sel[...] * (own - mean), axis=1, keepdims=True) for own in means]
    row = (row_index(size) % WINDOW_HEIGHT).astype(jnp.float32)
    column = lane_index(size).astype(jnp.float32)
    row = (row + 0.5 - WINDOW_HEIGHT / 2) / (WINDOW_HEIGHT / 2)
    column = (column + 0.5 - WINDOW_WIDTH / 2) / (WINDOW_WIDTH / 2)
    taper = (1.0 - row * row) * (1.0 - column * column) / (number - 1)
    for k in range(KINDS):
        cross = jnp.zeros((size, LANES), jnp.float32)
        for msg, shift in zip(msgs, shifts):
            cross = cross + msg[k * size : (k + 1) * size, :]
            cross = cross + shift * msg[part + k * size : part + (k + 1) * size, :]
        gain[k * size : (k + 1) * size, :] = taper * cross
    gain[part:, :] = jnp.zeros((8, LANES), jnp.float32)


def apply_kernel(cap, lat, lon, field, mine, theirs, weights, out, work, slots):
    members, _, rows, width = out.shape
    tiles = width // LANES
    size = cap * WINDOW_HEIGHT
    first = lax.axis_index("tile") * rows
    core = lax.axis_index("member") % 2
    count = find_slots(lat, slots, first, rows, cap)
    lane = lane_index()
    patch_row = row_index() < WINDOW_HEIGHT

    def add(layer_of_own):
        def one(s, carry):
            j = slots[s]
            row, block, after, shift = window(lat, lon, j, first, rows, tiles)
            here = patch_row & (lane >= shift)
            there = patch_row & (lane < shift)
            w = [weights[m, pl.ds(j, 1), :] for m in range(members)]
            for l, source in ((layer_of_own, mine), (1 - layer_of_own, theirs)):
                for k in range(KINDS):
                    gain = pltpu.roll(source[pl.ds(k * size + s * 4, 8), :], shift, 1)
                    near = jnp.where(here, gain, 0.0)
                    far = jnp.where(there, gain, 0.0)
                    for m in range(members):
                        f = m * FIELDS + l * KINDS + k
                        work[f, block, pl.ds(row, 8), :] += near * w[m]
                        work[f, after, pl.ds(row, 8), :] += far * w[m]
            return carry

        lax.fori_loop(0, count, one, 0)

    for c in range(2):
        pl.when(core == c)(functools.partial(add, c))
    for f in range(members * FIELDS):
        for i in range(tiles):
            out[f // FIELDS, f % FIELDS, :, i * LANES : (i + 1) * LANES] = work[f, i, PAD : PAD + rows, :]


def swaps(devices, row_tiles, start):
    routes = []
    for i in range(devices):
        for t in range(row_tiles):
            pair = t + 1 if (t - start) % 2 == 0 else t - 1
            to = (i, pair) if t >= start and pair < row_tiles else (i ^ 1, t)
            routes.append((i * row_tiles + t, to[0] * row_tiles + to[1]))
    return routes


def partner(size, k):
    if size & (size - 1) == 0:
        return [(i, i ^ k) for i in range(size)]
    return [(i, (i + k) % size) for i in range(size)]


def analyse(cap, shape, field, near, lat, lon, layer, kind, table, value, error, perturb):
    members, _, rows, width = shape
    row_tiles = lax.axis_size("tile")
    devices = lax.axis_size("member")
    chips = devices // 2
    both = 2 * members
    observations = lat.shape[0]
    size = cap * WINDOW_HEIGHT
    part = KINDS * size
    other_core = [(i, i ^ 1) for i in range(devices)]
    slots = pltpu.SMEM((cap + 1,), jnp.int32)
    (obs,) = call(
        functools.partial(observe_kernel, members),
        "observe",
        [SMEM] * 3 + [VMEM] * len(near),
        [(8, LANES)],
    )(layer, kind, table, *near)
    own, send, sel = call(
        functools.partial(cut_kernel, cap),
        "cut_patches",
        [SMEM] * 2 + [VMEM] * 2,
        [(members * part, LANES), (members * part + 8, LANES), (size, LANES)],
        [slots],
    )(lat, lon, field, obs)
    got = lax.ppermute(send, "member", other_core)
    (msg,) = call(
        functools.partial(pair_kernel, cap, members),
        "pair_moments",
        [VMEM] * 4,
        [(2 * part + 8, LANES)],
    )(own, got, obs, sel)
    msgs = [msg] + [lax.ppermute(msg, "member", partner(devices, 2 * k)) for k in range(1, chips)]
    mine, everyone = call(
        functools.partial(merge_kernel, cap, members, chips),
        "merge_moments",
        [VMEM] * (1 + chips),
        [(part + 8, LANES), (chips * both, LANES)],
    )(sel, *msgs)
    theirs = lax.ppermute(mine, "member", other_core)
    (weights,) = call(
        weight_kernel,
        "solve_weights",
        [SMEM] * 2 + [VMEM] * 2,
        [(members, observations, LANES)],
    )(value, error, perturb, everyone)
    analysed, _ = call(
        functools.partial(apply_kernel, cap),
        "apply_increments",
        [SMEM] * 2 + [VMEM] * 4,
        [shape, field.shape],
        [slots],
        aliases={2: 1},
    )(lat, lon, field, mine, theirs, weights)
    return analysed


def body(state, vel, band, table, lat, lon, layer, kind, value, error, perturb):
    members, _, rows, width = state.shape
    tiles = width // LANES
    row_tiles = lax.axis_size("tile")
    fields, parts = members * FIELDS, members * 2 * NLAYER
    padded_rows = rows + 2 * PAD
    caps = [cap for cap in CAPS if cap < lat.shape[0]] + [lat.shape[0]]
    message = (tiles * (parts + 2 * fields), LANES)
    out_a, out_b, near, s0, vs, bins = call(
        load_kernel,
        "load_arguments",
        [HBM] * 6,
        [
            (message[0] + NEAR_ROWS, LANES),
            message,
            (NEAR_ROWS, LANES),
            (fields, tiles + 2, padded_rows, LANES),
            (parts, tiles, padded_rows, LANES),
            jax.ShapeDtypeStruct((tiles, padded_rows, LANES), jnp.int32),
        ],
        [
            pltpu.SMEM(lat.shape, jnp.int32),
            pltpu.SMEM(lon.shape, jnp.int32),
            pltpu.SMEM(kind.shape, jnp.int32),
            pltpu.SemaphoreType.DMA((4 * members * tiles + tiles + 3,)),
        ],
    )(*held(lat, lon, kind, state, vel, band))
    devices = lax.axis_size("member")
    butterfly = row_tiles & (row_tiles - 1) == 0
    from_a = lax.ppermute(out_a, ("member", "tile"), swaps(devices, row_tiles, 0))
    from_b = lax.ppermute(out_b, ("member", "tile"), swaps(devices, row_tiles, 1))
    wide = pltpu.VMEM((fields, tiles + 2, padded_rows, LANES), jnp.float32)
    inner, own_edge, once_edge, vel_edge, bin_edge, step_of = call(
        functools.partial(interior_kernel, row_tiles, rows, caps[:-1]),
        "interior_rows",
        [HBM] * 2 + [VMEM] * 3,
        [
            (fields, tiles, padded_rows, LANES),
            (fields, tiles, 8, LANES),
            (fields, tiles, 8, LANES),
            (2, parts, tiles, 8, LANES),
            (tiles, 8, LANES),
            (1,),
        ],
        [
            wide,
            pltpu.SMEM(lat.shape, jnp.int32),
            pltpu.SMEM(table.shape, jnp.float32),
            pltpu.SemaphoreType.DMA((2,)),
        ],
        flops=20000000,
    )(*held(lat, table), s0, vs, bins)
    if butterfly:
        if row_tiles > 1:
            (near,) = call(combine_kernel, "combine_near", [VMEM] * 3, [(NEAR_ROWS, LANES)])(near, from_a, bin_edge)
        step = 2
        while step < row_tiles // 2:
            near = near + lax.ppermute(near, "tile", partner(row_tiles, step))
            step *= 2
        nears = [near] + ([lax.ppermute(near, "tile", partner(row_tiles, step))] if step < row_tiles else [])
    else:
        near = lax.psum(near, "tile")
        nears = [near]
    narrow = pltpu.VMEM((fields, tiles + 2, 8, LANES), jnp.float32)
    halo = pltpu.VMEM((message[0] + 2 * PAD, LANES), jnp.float32)
    (field,) = call(
        edge_kernel,
        "edge_rows",
        [SMEM] + [VMEM] * 8,
        [(fields, tiles, padded_rows, LANES)],
        [narrow, narrow, halo, halo],
        aliases={7: 0},
    )(table, own_edge, once_edge, vel_edge, bin_edge, from_a, from_b, inner, near)
    operands = (field, nears, lat, lon, layer, kind, table, value, error, perturb)
    return lax.switch(step_of[0], [functools.partial(analyse, cap, state.shape) for cap in caps], *operands)


def solution(mesh):
    placed = (
        P("member", None, "tile", None),
        P("member", None, "tile", None),
        P("tile", None),
        P(),
        P(),
        P(),
        P(),
        P(),
        P(),
        P(),
        P("member", None),
    )
    return jax.shard_map(
        body, mesh=mesh, in_specs=placed, out_specs=P("member", None, "tile", None), check_vma=False
    )
```

```python
import functools

import jax
import jax.numpy as jnp
from jax import lax
from jax.experimental import pallas as pl
from jax.experimental.pallas import tpu as pltpu
from jax.sharding import PartitionSpec as P

NLAYER = 2
NCLASS = 4
KINDS = NCLASS + 1
FIELDS = NLAYER * KINDS
WINDOW_HEIGHT = 4
WINDOW_WIDTH = 128
DIFFUSION = 0.08
DEPOSIT = 0.5
CAPS = (6, 7, 8, 10)

LANES = 128
PAD = 8
GROUP = 8
NEAR_ROWS = 48
EXACT = lax.Precision.HIGHEST
MIB = 1024 * 1024

SMEM = pl.BlockSpec(memory_space=pltpu.SMEM)
VMEM = pl.BlockSpec(memory_space=pltpu.VMEM)
HBM = pl.BlockSpec(memory_space=pltpu.HBM)


def call(kernel, name, in_specs, outs, scratch=(), flops=1000, aliases=None, limit=40, out_space=VMEM):
    return pl.pallas_call(
        kernel,
        name=name,
        in_specs=in_specs,
        out_specs=[SMEM if shape == (1,) else out_space for shape in outs],
        out_shape=[
            shape
            if isinstance(shape, jax.ShapeDtypeStruct)
            else jax.ShapeDtypeStruct(shape, jnp.int32 if shape == (1,) else jnp.float32)
            for shape in outs
        ],
        scratch_shapes=list(scratch),
        input_output_aliases=aliases or {},
        compiler_params=pltpu.CompilerParams(vmem_limit_bytes=limit * MIB),
        cost_estimate=pl.CostEstimate(flops=flops, bytes_accessed=1000, transcendentals=0),
    )


def held(*arrays):
    return [pltpu.with_memory_space_constraint(array, pltpu.HBM) for array in arrays]


def lane_index(rows=8):
    return lax.broadcasted_iota(jnp.int32, (rows, LANES), 1)


def row_index(rows=8):
    return lax.broadcasted_iota(jnp.int32, (rows, LANES), 0)


def spread(ref, group, rows=8):
    index = lane_index(rows) // group
    total = jnp.zeros((rows, LANES), ref.dtype)
    for j in range(ref.shape[0]):
        total = jnp.where(index == j, ref[j], total)
    return total


def find_slots(lat, slots, first, rows, cap):
    for s in range(cap + 1):
        slots[s] = 0
    count = jnp.int32(0)
    for j in range(lat.shape[0]):
        start = lat[j] - WINDOW_HEIGHT // 2 - first
        slots[jnp.minimum(count, cap)] = j
        count = count + ((start < rows) & (start + WINDOW_HEIGHT > 0)).astype(jnp.int32)
    return jnp.minimum(count, cap)


def window(lat, lon, j, first, rows, tiles):
    row = jnp.clip(lat[j] - WINDOW_HEIGHT // 2 - first, -WINDOW_HEIGHT, rows) + PAD
    left = lon[j] - WINDOW_WIDTH // 2
    block = left // LANES
    return row, block, jnp.minimum(block + 1, tiles - 1), left % LANES


def coefficients(u, w):
    return (
        (1.0 - 4.0 * DIFFUSION) - (jnp.abs(u) + jnp.abs(w)),
        jnp.maximum(u, 0.0) + DIFFUSION,
        DIFFUSION - jnp.minimum(u, 0.0),
        jnp.maximum(w, 0.0) + DIFFUSION,
        DIFFUSION - jnp.minimum(w, 0.0),
    )


def stencil(coef, centre, up, down, left, right):
    return (coef[0] * centre + coef[1] * up) + (coef[2] * down + coef[3] * left) + coef[4] * right


def choose(values, pick):
    total = jnp.zeros((values.shape[0], LANES), jnp.float32)
    for _ in range(3):
        part = values.astype(jnp.bfloat16)
        total = total + jnp.dot(part, pick, preferred_element_type=jnp.float32)
        values = values - part.astype(jnp.float32)
    return total


def lane_tiles(source, target, members, tiles, each, rows, shift):
    return [
        (
            source.at[m, :, :, pl.ds(i * LANES, LANES)],
            target.at[pl.ds(m * each, each), i + shift, pl.ds(PAD, rows), :],
        )
        for m in range(members)
        for i in range(tiles)
    ]


def start_copies(moves, sems):
    copies = [pltpu.make_async_copy(src, dst, sems.at[n]) for n, (src, dst) in enumerate(moves)]
    for copy in copies:
        copy.start()
    return copies


def load_kernel(lat_hbm, lon_hbm, kind_hbm, state_hbm, vel_hbm, band_hbm, out_a, out_b, near, s0, vs, bs, lat, lon, kind, sems):
    members, _, rows, width = state_hbm.shape
    tiles = width // LANES
    fields, parts = members * FIELDS, members * 2 * NLAYER
    moves = lane_tiles(state_hbm, s0, members, tiles, FIELDS, rows, 1)
    moves += lane_tiles(vel_hbm, vs, members, tiles, 2 * NLAYER, rows, 0)
    moves += [(band_hbm.at[:, pl.ds(i * LANES, LANES)], bs.at[i, pl.ds(PAD, rows), :]) for i in range(tiles)]
    moves += [(lat_hbm, lat), (lon_hbm, lon), (kind_hbm, kind)]
    copies = start_copies(moves, sems)
    tile = lax.axis_index("tile")
    first = tile * rows
    even = tile % 2 == 0
    zero = jnp.zeros((PAD, LANES), jnp.float32)
    bands = jnp.zeros((PAD, LANES), jnp.int32)
    for i in range(tiles):
        for part in (slice(0, PAD), slice(PAD + rows, None)):
            for f in range(fields):
                s0[f, i + 1, part, :] = zero
            for c in range(parts):
                vs[c, i, part, :] = zero
            bs[i, part, :] = bands
    for f in range(fields):
        for r in range(0, rows + 2 * PAD, PAD):
            s0[f, 0, r : r + PAD, :] = zero
            s0[f, tiles + 1, r : r + PAD, :] = zero
    for copy in copies:
        copy.wait()

    def edge(out, q_first, v_at):
        for i in range(tiles):
            for c in range(parts):
                to = i * parts + c
                out[to : to + 1, :] = vs[c, i, v_at : v_at + 1, :]
            for f in range(fields):
                to = tiles * parts + (i * fields + f) * 2
                out[to : to + 2, :] = s0[f, i + 1, q_first : q_first + 2, :]

    top, bottom = PAD, PAD + rows

    @pl.when(even)
    def _():
        edge(out_a, bottom - 2, bottom - 1)
        edge(out_b, top, top)

    @pl.when(jnp.logical_not(even))
    def _():
        edge(out_a, top, top)
        edge(out_b, bottom - 2, bottom - 1)

    lane = lane_index()
    row = row_index()
    blank = jnp.zeros((8, LANES), jnp.float32)
    pairs = members * NLAYER
    qs, us, ws, bins = [blank] * pairs, [blank] * pairs, [blank] * pairs, blank
    for j in range(lat.shape[0]):
        start = jnp.clip(lat[j] - 2 - first, -PAD, rows) + PAD
        left = lon[j] - 2
        block, shift = left // LANES, left % LANES
        after = jnp.minimum(block + 1, tiles - 1)
        turn = (GROUP * j - shift + LANES) % LANES
        here = lane >= shift
        mine = (lane // GROUP) == j

        def fetch(ref, old, *lead, by=0):
            both = jnp.where(
                here, ref[lead + (block + by, pl.ds(start, 8))], ref[lead + (after + by, pl.ds(start, 8))]
            )
            return jnp.where(mine, pltpu.roll(both.astype(jnp.float32), turn, 1), old)

        for m in range(members):
            for l in range(NLAYER):
                s = m * NLAYER + l
                qs[s] = fetch(s0, qs[s], m * FIELDS + l * KINDS + kind[j], by=1)
                us[s] = fetch(vs, us[s], 2 * s)
                ws[s] = fetch(vs, ws[s], 2 * s + 1)
        bins = fetch(bs, bins)

    blocks = [jnp.where(row < 5, q, pltpu.roll(u, 4, 0)) for q, u in zip(qs, us)]
    for m in range(members):
        w = jnp.where(row < 4, ws[2 * m], pltpu.roll(ws[2 * m + 1], 4, 0))
        blocks.append(jnp.where(row == 0, pltpu.roll(bins, 6, 0), w))
    for n, block in enumerate(blocks):
        near[8 * n : 8 * n + 8, :] = block
        base = tiles * (parts + 2 * fields) + 8 * n
        out_a[base : base + 8, :] = block


def combine_kernel(near, from_a, _, out):
    out[...] = near[...] + from_a[from_a.shape[0] - NEAR_ROWS :, :]


def advance(source, f, i, r, coef, lane):
    centre = source[f, i + 1, r : r + 8, :]
    up = source[f, i + 1, r - 1 : r + 7, :]
    down = source[f, i + 1, r + 1 : r + 9, :]
    left, right = sides_of(source[f, i, r : r + 8, :], centre, source[f, i + 2, r : r + 8, :], lane)
    return stencil(coef, centre, up, down, left, right)


def sides_of(before, centre, after, lane):
    left = pltpu.roll(jnp.where(lane == LANES - 1, before, centre), 1, 1)
    right = pltpu.roll(jnp.where(lane == 0, after, centre), LANES - 1, 1)
    return left, right


def settle(a, b, bins, table, k):
    if k == 0:
        return a, b
    rate = jnp.full(a.shape, table[0, k - 1], jnp.float32)
    for level in range(1, table.shape[0]):
        rate = jnp.where(bins == level, table[level, k - 1], rate)
    settled = rate * a
    return a - settled, b + settled - DEPOSIT * rate * b


def interior_kernel(row_tiles, rows, caps, lat_hbm, table_hbm, s0, vs, band, padded, own_edge, once_edge, vel_edge, bin_edge, step_of, s1, lat, table, sems):
    fields, tiles, _, _ = padded.shape
    members = fields // FIELDS
    parts = members * 2 * NLAYER
    copies = start_copies([(lat_hbm, lat), (table_hbm, table)], sems)
    zero = jnp.zeros((rows + 2 * PAD, LANES), jnp.float32)
    lane = lane_index()
    for f in range(fields):
        s1[f, 0, :, :] = zero
        s1[f, tiles + 1, :, :] = zero

    def first_step(t, carry):
        ml, i = t // tiles, t % tiles
        for r in range(PAD, PAD + rows, 8):
            coef = coefficients(vs[2 * ml, i, r : r + 8, :], vs[2 * ml + 1, i, r : r + 8, :])
            for k in range(KINDS):
                s1[ml * KINDS + k, i + 1, r : r + 8, :] = advance(s0, ml * KINDS + k, i, r, coef, lane)
        return carry

    for t in range(members * NLAYER * tiles):
        first_step(t, 0)
    for copy in copies:
        copy.wait()

    most = jnp.int32(0)
    for n in range(row_tiles):
        count = jnp.int32(0)
        for j in range(lat.shape[0]):
            start = lat[j] - WINDOW_HEIGHT // 2 - n * rows
            count = count + ((start < rows) & (start + WINDOW_HEIGHT > 0)).astype(jnp.int32)
        most = jnp.maximum(most, count)
    step_of[0] = sum((most > cap).astype(jnp.int32) for cap in caps)

    def second_step(t, carry):
        m, i = t // tiles, t % tiles
        for r in range(PAD, PAD + rows, 8):
            coefs = []
            for l in range(NLAYER):
                mc = (m * NLAYER + l) * 2
                coefs.append(coefficients(vs[mc, i, r : r + 8, :], vs[mc + 1, i, r : r + 8, :]))
            bins = band[i, r : r + 8, :]
            for k in range(KINDS):
                upper = m * FIELDS + k
                lower = upper + KINDS
                a = advance(s1, upper, i, r, coefs[0], lane)
                b = advance(s1, lower, i, r, coefs[1], lane)
                a, b = settle(a, b, bins, table, k)
                padded[upper, i, r : r + 8, :] = a
                padded[lower, i, r : r + 8, :] = b
        return carry

    for t in range(members * tiles):
        second_step(t, 0)

    top, bottom = PAD, PAD + rows
    half = row_index() < 4

    def halves(ref, lead, low, high):
        return jnp.where(half, ref[lead + (slice(low, low + 8), slice(None))], ref[lead + (slice(high - 4, high + 4), slice(None))])

    for i in range(tiles):
        for f in range(fields):
            padded[f, i, :PAD, :] = zero[:PAD]
            padded[f, i, PAD + rows :, :] = zero[:PAD]
            own_edge[f, i, :, :] = halves(s0, (f, i + 1), top - 2, bottom - 2)
            once_edge[f, i, :, :] = halves(s1, (f, i + 1), top - 1, bottom - 3)
        for c in range(parts):
            vel_edge[0, c, i, :, :] = halves(vs, (c, i), top - 2, bottom - 2)
            vel_edge[1, c, i, :, :] = halves(vs, (c, i), top - 1, bottom - 3)
        bin_edge[i, :, :] = halves(band, (i,), top - 1, bottom - 3).astype(jnp.float32)


def observe_kernel(members, layer, kind, table, *rest):
    parts, out = rest[:-1], rest[-1]
    pairs = members * NLAYER
    blocks = []
    for n in range(pairs + members):
        block = parts[0][8 * n : 8 * n + 8, :]
        for more in parts[1:]:
            block = block + more[8 * n : 8 * n + 8, :]
        blocks.append(block)
    bins = jnp.broadcast_to(blocks[pairs][:1], (8, LANES))
    kinds = spread(kind, GROUP)
    layers = spread(layer, GROUP)
    rate = jnp.zeros((8, LANES), jnp.float32)
    for level in range(table.shape[0]):
        here = jnp.abs(bins - level) < 0.5
        for k in range(NCLASS):
            rate = jnp.where(here & (kinds == k + 1), table[level, k], rate)
    row = row_index()

    def step(q, coef):
        return stencil(
            coef,
            q,
            pltpu.roll(q, 1, 0),
            pltpu.roll(q, 7, 0),
            pltpu.roll(q, 1, 1),
            pltpu.roll(q, LANES - 1, 1),
        )

    seen = jnp.zeros((8, LANES), jnp.float32)
    for m in range(members):
        values = []
        for l in range(NLAYER):
            q = blocks[m * NLAYER + l]
            u = pltpu.roll(q, 4, 0)
            w = blocks[pairs + m]
            coef = coefficients(u, w if l == 0 else pltpu.roll(w, 4, 0))
            values.append(step(step(q, coef), coef))
        a, b = values
        settled = rate * a
        value = jnp.where(layers == 0, a - settled, b + settled - DEPOSIT * rate * b)
        seen = jnp.where(row == m, pltpu.roll(value, (m - 2) % 8, 0), seen)
    squeeze = (
        lax.broadcasted_iota(jnp.int32, (LANES, LANES), 0)
        == lax.broadcasted_iota(jnp.int32, (LANES, LANES), 1) * GROUP + 2
    ).astype(jnp.bfloat16)
    out[...] = choose(seen, squeeze)


def edge_kernel(table, own_edge, once_edge, vel_edge, bin_edge, from_a, from_b, inner, near, padded, e0, e1, up, down):
    fields, tiles, padded_rows, _ = padded.shape
    rows = padded_rows - 2 * PAD
    members = fields // FIELDS
    parts = members * 2 * NLAYER
    tile = lax.axis_index("tile")
    count_tiles = lax.axis_size("tile")
    even = tile % 2 == 0
    sent = from_b.shape[0]

    @pl.when(even)
    def _():
        down[PAD : PAD + sent, :] = from_a[:sent, :]
        up[PAD : PAD + sent, :] = from_b[...]

    @pl.when(jnp.logical_not(even))
    def _():
        up[PAD : PAD + sent, :] = from_a[:sent, :]
        down[PAD : PAD + sent, :] = from_b[...]

    for edge_tile, ref in ((0, up), (count_tiles - 1, down)):

        @pl.when(tile == edge_tile)
        def _():
            ref[...] = jnp.zeros(ref.shape, jnp.float32)

    lane = lane_index()
    row = row_index()
    zero = jnp.zeros((8, LANES), jnp.float32)
    v_base = PAD
    q_base = PAD + tiles * parts
    for f in range(fields):
        for buffer in (e0, e1):
            buffer[f, 0, :, :] = zero
            buffer[f, tiles + 1, :, :] = zero

    def gather(i, carry):
        for f in range(fields):
            at = q_base + (i * fields + f) * 2
            q = jnp.where(row < 2, up[pl.ds(at, 8), :], own_edge[f, i, :, :])
            e0[f, i + 1, :, :] = jnp.where(row > 5, down[pl.ds(at - 6, 8), :], q)
        return carry

    for i in range(tiles):
        gather(i, 0)
    outside = ((row == 0) & (tile == 0)) | ((row == 7) & (tile == count_tiles - 1))

    def first_step(t, carry):
        ml, i = t // tiles, t % tiles
        flow = []
        for c in range(2):
            at = v_base + i * parts + 2 * ml + c
            v = jnp.where(row == 1, up[pl.ds(at - 1, 8), :], vel_edge[0, 2 * ml + c, i, :, :])
            flow.append(jnp.where(row == 6, down[pl.ds(at - 6, 8), :], v))
        coef = coefficients(*flow)
        for k in range(KINDS):
            f = ml * KINDS + k
            centre = e0[f, i + 1, :, :]
            left, right = sides_of(e0[f, i, :, :], centre, e0[f, i + 2, :, :], lane)
            q = stencil(coef, centre, pltpu.roll(centre, 1, 0), pltpu.roll(centre, 7, 0), left, right)
            q = jnp.where(row < 2, pltpu.roll(q, 7, 0), jnp.where(row > 5, pltpu.roll(q, 1, 0), once_edge[f, i, :, :]))
            e1[f, i + 1, :, :] = jnp.where(outside, 0.0, q)
        return carry

    for t in range(members * NLAYER * tiles):
        first_step(t, 0)

    def second_step(t, carry):
        m, i = t // tiles, t % tiles
        bins = bin_edge[i, :, :].astype(jnp.int32)
        values = []
        for l in range(NLAYER):
            mc = (m * NLAYER + l) * 2
            coef = coefficients(vel_edge[1, mc, i, :, :], vel_edge[1, mc + 1, i, :, :])
            for k in range(KINDS):
                f = m * FIELDS + l * KINDS + k
                centre = e1[f, i + 1, :, :]
                left, right = sides_of(e1[f, i, :, :], centre, e1[f, i + 2, :, :], lane)
                values.append(
                    stencil(coef, centre, pltpu.roll(centre, 1, 0), pltpu.roll(centre, 7, 0), left, right)
                )
        for k in range(KINDS):
            for l, q in enumerate(settle(values[k], values[KINDS + k], bins, table, k)):
                f = m * FIELDS + l * KINDS + k
                padded[f, i, PAD : PAD + 2, :] = q[1:3]
                padded[f, i, PAD + rows - 2 : PAD + rows, :] = q[5:7]
        return carry

    for t in range(members * tiles):
        second_step(t, 0)


def cut_kernel(cap, lat, lon, padded, obs, own, send, sel, slots):
    fields, tiles, padded_rows, _ = padded.shape
    rows = padded_rows - 2 * PAD
    members = fields // FIELDS
    core = lax.axis_index("member") % 2
    first = lax.axis_index("tile") * rows
    lane = lane_index()
    size = cap * WINDOW_HEIGHT
    count = find_slots(lat, slots, first, rows, cap)
    for s in range(cap):
        sel[s * 4 : s * 4 + 4, :] = (lane[:4] == slots[s]).astype(jnp.float32)
    send[members * KINDS * size :, :] = obs[...]

    def cut(layer_of_own):
        def one(s, carry):
            row, block, after, shift = window(lat, lon, slots[s], first, rows, tiles)
            here = lane >= shift
            for l, target in ((layer_of_own, own), (1 - layer_of_own, send)):
                for m in range(members):
                    for k in range(KINDS):
                        f = m * FIELDS + l * KINDS + k
                        both = jnp.where(
                            here, padded[f, block, pl.ds(row, 8), :], padded[f, after, pl.ds(row, 8), :]
                        )
                        patch = pltpu.roll(both, (LANES - shift) % LANES, 1)
                        target[pl.ds((m * KINDS + k) * size + s * 4, 4), :] = patch[:4]
            return carry

        lax.fori_loop(0, count, one, 0)

    for c in range(2):
        pl.when(core == c)(functools.partial(cut, c))


def pair_kernel(cap, members, halves, own, got, obs, sel, *msgs):
    size = cap * WINDOW_HEIGHT
    part = KINDS * size
    seen, theirs = obs[:members, :], got[members * part : members * part + members, :]
    mean = (jnp.sum(seen, axis=0, keepdims=True) + jnp.sum(theirs, axis=0, keepdims=True)) / (2 * members)
    sources = [(own, m, seen[m : m + 1]) for m in range(members)]
    sources += [(got, m, theirs[m : m + 1]) for m in range(members)]
    weight = [jnp.sum(sel[...] * (o - mean), axis=1, keepdims=True) for _, _, o in sources]
    for kinds, msg in zip(halves, msgs):
        sums = len(kinds) * size
        for n, k in enumerate(kinds):
            cross = jnp.zeros((size, LANES), jnp.float32)
            total = jnp.zeros((size, LANES), jnp.float32)
            for (ref, m, _), o in zip(sources, weight):
                patch = ref[m * part + k * size : m * part + (k + 1) * size, :]
                cross = cross + patch * o
                total = total + patch
            msg[n * size : (n + 1) * size, :] = cross
            msg[sums + n * size : sums + (n + 1) * size, :] = total
        msg[2 * sums :, :] = jnp.zeros((msg.shape[0] - 2 * sums, LANES), jnp.float32)
        msg[2 * sums : 2 * sums + members, :] = seen
        msg[2 * sums + members : 2 * sums + 2 * members, :] = theirs


def joined(size, count, seen, sel, mine, theirs, n, sums):
    def mean(ref):
        return jnp.sum(ref[2 * sums : 2 * sums + seen, :], axis=0, keepdims=True) / seen

    shift = jnp.sum(sel[...] * (0.5 * (mean(mine) - mean(theirs))), axis=1, keepdims=True)
    at, low = slice(n * size, (n + 1) * size), slice(sums + n * size, sums + (n + 1) * size)
    return mine[at, :] + theirs[at, :] + shift * (mine[low, :] - theirs[low, :])


def join_kernel(size, count, seen, sel, mine, theirs, out):
    sums = count * size
    for n in range(count):
        low = slice(sums + n * size, sums + (n + 1) * size)
        out[n * size : (n + 1) * size, :] = joined(size, count, seen, sel, mine, theirs, n, sums)
        out[low, :] = mine[low, :] + theirs[low, :]
    base = 2 * sums
    out[base:, :] = jnp.zeros((out.shape[0] - base, LANES), jnp.float32)
    out[base : base + seen, :] = mine[base : base + seen, :]
    out[base + seen : base + 2 * seen, :] = theirs[base : base + seen, :]


def weight_kernel(value, error, perturb, everyone_ref, weights):
    members, observations = perturb.shape
    everyone = everyone_ref[...]
    number = everyone.shape[0]
    anomaly = everyone - jnp.sum(everyone, axis=0, keepdims=True) / number
    over = (((0,), (0,)), ((), ()))
    cov = lax.dot_general(anomaly, anomaly, over, precision=EXACT, preferred_element_type=jnp.float32)
    row16 = row_index(observations)
    lane16 = lane_index(observations)
    errors = spread(error, 1)
    innovation = spread(value, 1)[:members] - everyone[:members]
    noise = jnp.concatenate(
        [perturb[...], jnp.zeros((members, LANES - observations), jnp.float32)], axis=1
    )
    innovation = innovation + jnp.sqrt(errors[:members]) * noise
    place = (lane_index(members) == row_index(members) + observations).astype(jnp.float32)
    sides = lax.dot_general(innovation, place, over, precision=EXACT, preferred_element_type=jnp.float32)
    system = jnp.where(lane16 < observations, cov[:observations] / (number - 1), sides[:observations])
    system = system + jnp.where(lane16 == row16, jnp.broadcast_to(errors[:1], row16.shape), 0.0)
    for k in range(observations):
        pivot = system[k : k + 1, :] / system[k : k + 1, k : k + 1]
        system = jnp.where(row16 == k, pivot, system - system[:, k : k + 1] * pivot)
    for m in range(members):
        weights[m, :, :] = jnp.broadcast_to(
            system[:, observations + m : observations + m + 1], (observations, LANES)
        )


def merge_kernel(cap, halves, seen, sel, *rest):
    pairs, (gain, everyone) = rest[:-2], rest[-2:]
    size = cap * WINDOW_HEIGHT
    number = 2 * seen
    row = (row_index(size) % WINDOW_HEIGHT).astype(jnp.float32)
    column = lane_index(size).astype(jnp.float32)
    row = (row + 0.5 - WINDOW_HEIGHT / 2) / (WINDOW_HEIGHT / 2)
    column = (column + 0.5 - WINDOW_WIDTH / 2) / (WINDOW_WIDTH / 2)
    taper = (1.0 - row * row) * (1.0 - column * column) / (number - 1)
    for h, kinds in enumerate(halves):
        mine, theirs = pairs[2 * h : 2 * h + 2]
        sums = len(kinds) * size
        if h == 0:
            everyone[:seen, :] = mine[2 * sums : 2 * sums + seen, :]
            everyone[seen:, :] = theirs[2 * sums : 2 * sums + seen, :]
        for n, k in enumerate(kinds):
            cross = joined(size, len(kinds), seen, sel, mine, theirs, n, sums)
            gain[k * size : (k + 1) * size, :] = taper * cross
    gain[KINDS * size :, :] = jnp.zeros((8, LANES), jnp.float32)


def apply_kernel(cap, lat, lon, field, mine, theirs, weights, out, work, slots):
    members, _, rows, width = out.shape
    tiles = width // LANES
    size = cap * WINDOW_HEIGHT
    first = lax.axis_index("tile") * rows
    core = lax.axis_index("member") % 2
    count = find_slots(lat, slots, first, rows, cap)
    lane = lane_index()
    patch_row = row_index() < WINDOW_HEIGHT

    def add(layer_of_own):
        def one(s, carry):
            j = slots[s]
            row, block, _, shift = window(lat, lon, j, first, rows, tiles)
            after = (block + 1) % tiles
            here = patch_row & (lane >= shift)
            there = patch_row & (lane < shift)
            w = [weights[m, pl.ds(j, 1), :] for m in range(members)]
            for l, source in ((layer_of_own, mine), (1 - layer_of_own, theirs)):
                gains = [pltpu.roll(source[pl.ds(k * size + s * 4, 8), :], shift, 1) for k in range(KINDS)]
                new = []
                for m in range(members):
                    for k in range(KINDS):
                        f = m * FIELDS + l * KINDS + k
                        change = gains[k] * w[m]
                        for at, part in ((block, here), (after, there)):
                            new.append((f, at, work[f, at, pl.ds(row, 8), :] + jnp.where(part, change, 0.0)))
                for f, at, value in new:
                    work[f, at, pl.ds(row, 8), :] = value
            return carry

        lax.fori_loop(0, count, one, 0)

    for c in range(2):
        pl.when(core == c)(functools.partial(add, c))
    for f in range(members * FIELDS):
        for i in range(tiles):
            out[f // FIELDS, f % FIELDS, :, i * LANES : (i + 1) * LANES] = work[f, i, PAD : PAD + rows, :]


def swaps(devices, row_tiles, start):
    routes = []
    for i in range(devices):
        for t in range(row_tiles):
            pair = t + 1 if (t - start) % 2 == 0 else t - 1
            to = (i, pair) if t >= start and pair < row_tiles else (i ^ 1, t)
            routes.append((i * row_tiles + t, to[0] * row_tiles + to[1]))
    return routes


def partner(size, k):
    if size & (size - 1) == 0:
        return [(i, i ^ k) for i in range(size)]
    return [(i, (i + k) % size) for i in range(size)]


def analyse(cap, shape, field, near, lat, lon, layer, kind, table, value, error, perturb):
    members, _, rows, width = shape
    row_tiles = lax.axis_size("tile")
    devices = lax.axis_size("member")
    chips = devices // 2
    both = 2 * members
    observations = lat.shape[0]
    size = cap * WINDOW_HEIGHT
    part = KINDS * size
    other_core = [(i, i ^ 1) for i in range(devices)]
    slots = pltpu.SMEM((cap + 1,), jnp.int32)
    (obs,) = call(
        functools.partial(observe_kernel, members),
        "observe",
        [SMEM] * 3 + [VMEM] * len(near),
        [(8, LANES)],
    )(layer, kind, table, *near)
    own, send, sel = call(
        functools.partial(cut_kernel, cap),
        "cut_patches",
        [SMEM] * 2 + [VMEM] * 2,
        [(members * part, LANES), (members * part + 8, LANES), (size, LANES)],
        [slots],
    )(lat, lon, field, obs)
    got = lax.ppermute(send, "member", other_core)
    halves = (tuple(range((KINDS + 1) // 2)), tuple(range((KINDS + 1) // 2, KINDS)))
    seen_rows = -(-chips * both // 8) * 8
    msgs = call(
        functools.partial(pair_kernel, cap, members, halves),
        "pair_moments",
        [VMEM] * 4,
        [(2 * len(kinds) * size + seen_rows, LANES) for kinds in halves],
    )(own, got, obs, sel)
    steps = [1 << n for n in range(1, devices.bit_length() - 1)]
    seen = both
    for n in range(len(steps)):
        others = [
            lax.ppermute(msg, "member", partner(devices, steps[(n + h) % len(steps)]))
            for h, msg in enumerate(msgs)
        ]
        if n == len(steps) - 1:
            break
        msgs = [
            call(
                functools.partial(join_kernel, size, len(kinds), seen),
                "join_moments",
                [VMEM] * 3,
                [msg.shape],
            )(sel, msg, other)[0]
            for kinds, msg, other in zip(halves, msgs, others)
        ]
        seen *= 2
    mine, everyone = call(
        functools.partial(merge_kernel, cap, halves, seen),
        "merge_moments",
        [VMEM] * 5,
        [(part + 8, LANES), (chips * both, LANES)],
    )(sel, msgs[0], others[0], msgs[1], others[1])
    theirs = lax.ppermute(mine, "member", other_core)
    (weights,) = call(
        weight_kernel,
        "solve_weights",
        [SMEM] * 2 + [VMEM] * 2,
        [(members, observations, LANES)],
    )(value, error, perturb, everyone)
    analysed, _ = call(
        functools.partial(apply_kernel, cap),
        "apply_increments",
        [SMEM] * 2 + [VMEM] * 4,
        [shape, field.shape],
        [slots],
        aliases={2: 1},
    )(lat, lon, field, mine, theirs, weights)
    return analysed


def body(state, vel, band, table, lat, lon, layer, kind, value, error, perturb):
    members, _, rows, width = state.shape
    tiles = width // LANES
    row_tiles = lax.axis_size("tile")
    fields, parts = members * FIELDS, members * 2 * NLAYER
    padded_rows = rows + 2 * PAD
    caps = [cap for cap in CAPS if cap < lat.shape[0]] + [lat.shape[0]]
    message = (tiles * (parts + 2 * fields), LANES)
    out_a, out_b, near, s0, vs, bins = call(
        load_kernel,
        "load_arguments",
        [HBM] * 6,
        [
            (message[0] + NEAR_ROWS, LANES),
            message,
            (NEAR_ROWS, LANES),
            (fields, tiles + 2, padded_rows, LANES),
            (parts, tiles, padded_rows, LANES),
            jax.ShapeDtypeStruct((tiles, padded_rows, LANES), jnp.int32),
        ],
        [
            pltpu.SMEM(lat.shape, jnp.int32),
            pltpu.SMEM(lon.shape, jnp.int32),
            pltpu.SMEM(kind.shape, jnp.int32),
            pltpu.SemaphoreType.DMA((4 * members * tiles + tiles + 3,)),
        ],
    )(*held(lat, lon, kind, state, vel, band))
    devices = lax.axis_size("member")
    butterfly = row_tiles & (row_tiles - 1) == 0
    from_a = lax.ppermute(out_a, ("member", "tile"), swaps(devices, row_tiles, 0))
    from_b = lax.ppermute(out_b, ("member", "tile"), swaps(devices, row_tiles, 1))
    wide = pltpu.VMEM((fields, tiles + 2, padded_rows, LANES), jnp.float32)
    inner, own_edge, once_edge, vel_edge, bin_edge, step_of = call(
        functools.partial(interior_kernel, row_tiles, rows, caps[:-1]),
        "interior_rows",
        [HBM] * 2 + [VMEM] * 3,
        [
            (fields, tiles, padded_rows, LANES),
            (fields, tiles, 8, LANES),
            (fields, tiles, 8, LANES),
            (2, parts, tiles, 8, LANES),
            (tiles, 8, LANES),
            (1,),
        ],
        [
            wide,
            pltpu.SMEM(lat.shape, jnp.int32),
            pltpu.SMEM(table.shape, jnp.float32),
            pltpu.SemaphoreType.DMA((2,)),
        ],
        flops=20000000,
    )(*held(lat, table), s0, vs, bins)
    if butterfly:
        if row_tiles > 1:
            (near,) = call(combine_kernel, "combine_near", [VMEM] * 3, [(NEAR_ROWS, LANES)])(near, from_a, bin_edge)
        step = 2
        while step < row_tiles // 2:
            near = near + lax.ppermute(near, "tile", partner(row_tiles, step))
            step *= 2
        nears = [near] + ([lax.ppermute(near, "tile", partner(row_tiles, step))] if step < row_tiles else [])
    else:
        near = lax.psum(near, "tile")
        nears = [near]
    narrow = pltpu.VMEM((fields, tiles + 2, 8, LANES), jnp.float32)
    halo = pltpu.VMEM((message[0] + 2 * PAD, LANES), jnp.float32)
    (field,) = call(
        edge_kernel,
        "edge_rows",
        [SMEM] + [VMEM] * 8,
        [(fields, tiles, padded_rows, LANES)],
        [narrow, narrow, halo, halo],
        aliases={7: 0},
    )(table, own_edge, once_edge, vel_edge, bin_edge, from_a, from_b, inner, near)
    operands = (field, nears, lat, lon, layer, kind, table, value, error, perturb)
    return lax.switch(step_of[0], [functools.partial(analyse, cap, state.shape) for cap in caps], *operands)


def solution(mesh):
    placed = (
        P("member", None, "tile", None),
        P("member", None, "tile", None),
        P("tile", None),
        P(),
        P(),
        P(),
        P(),
        P(),
        P(),
        P(),
        P("member", None),
    )
    return jax.shard_map(
        body, mesh=mesh, in_specs=placed, out_specs=P("member", None, "tile", None), check_vma=False
    )
```
